1024 devices in a mesh: context: 64 (over x, z_hi, y), tensor: 16 (over z_lo, core).
Axes of the slice: x: 4, y: 4, z: 32 (z_hi: 4, z_lo: 8; z = z_hi * 8 + z_lo), core: 2. Of those that a mesh axis runs over, the one named last changes fastest.
Arguments:
- features: bfloat16 [3, 4096, 16384], P(None, 'tensor', 'context'), may hold values from -6 to 6
- short_taps: float32 [3, 3, 4096], P(None, None, 'tensor'), may hold values from -3 to 3
- long_filter: bfloat16 [4096, 16384], P('tensor', 'context'), may hold values from -2 to 2, as said below
- skip_bias: float32 [4096], P('tensor'), may hold values from 0.5 to 1.5
- out_weight: bfloat16 [4096, 4096], P('tensor'), may hold values from -0.125 to 0.125
Outputs:
- layer_out: bfloat16 [16384, 4096], P('context', 'tensor')
The draws below stay inside these ranges and needn't reach their ends.
Inputs may be any that keep to these rules, and one draw needn't show every extreme that they name: `long_filter`: taps of the implicit filter.
All inputs are finite; a program needn't handle non-finite values.
Results may differ from the reference program's by a relative error of at most 0.007.
Values may be sent and summed in bfloat16 or wider, within the bound.
A program may use at most 32 MiB of HBM per device.

```python
import math
import jax
import jax.numpy as jnp
from jax import lax

KERNEL_FEATURES = 4096
OUT_WIDTH = 4096
TAPS = 3
TOKEN_COUNT = 16384


def draw_long_filter(key, part):
    key = jax.random.fold_in(key, 11)
    fading_rate_seed, spike_seed, masking_seed, magnitude_seed = jax.random.split(key, 4)
    log_tau = jax.random.uniform(fading_rate_seed, (KERNEL_FEATURES, 1), jnp.float32, math.log(30.0), math.log(4.0 * TOKEN_COUNT))
    tau_len = jnp.exp(log_tau)
    kernel_offsets = jnp.arange(TOKEN_COUNT, dtype=jnp.float32)[None, :]
    spike_offsets = jax.random.randint(spike_seed, (KERNEL_FEATURES, 4), 1, TOKEN_COUNT).astype(jnp.float32)
    zeroed_offsets = jax.random.uniform(masking_seed, (KERNEL_FEATURES, 4), jnp.float32, 0.5, 0.8)
    fading_profile = jnp.exp(-kernel_offsets / tau_len)
    for chosen_feature in range(4):
        fading_profile = fading_profile * jnp.where(kernel_offsets >= spike_offsets[:, chosen_feature:chosen_feature + 1], zeroed_offsets[:, chosen_feature:chosen_feature + 1], 1.0)
    scale_amp = jnp.sqrt(2.0 / jnp.minimum(tau_len, float(TOKEN_COUNT)))
    amplitude = jnp.clip(jax.random.normal(magnitude_seed, (KERNEL_FEATURES, TOKEN_COUNT), jnp.float32), -4.0, 4.0)
    return (amplitude * scale_amp * fading_profile).astype(jnp.bfloat16)


def with_spikes(drawn, rng, source, target, blocks, factor):
    owner, partner = [(jnp.arange(drawn.shape[axis_at]) // (drawn.shape[axis_at] // blocks)).reshape([-1 if axis == axis_at else 1 for axis in range(drawn.ndim)]) for axis_at in (source, target)]
    chosen = jax.random.permutation(rng, blocks)[partner]
    strong = (owner == chosen) | (owner == (partner + blocks // 2) % blocks)
    return jnp.where(strong, factor * drawn, drawn)


def steps_of(rng, shape, cuts, least, top_value):
    gain, own = 1.0, jax.random.fold_in(rng, 6)
    for axis_at, blocks in cuts:
        heights = jnp.exp(jax.random.uniform(jax.random.fold_in(own, axis_at), (blocks,), jnp.float32, least / len(cuts), top_value / len(cuts)))
        gain = gain * jnp.repeat(heights, shape[axis_at] // blocks).reshape([-1 if axis == axis_at else 1 for axis in range(len(shape))])
    return gain


def scatter_about(own_key, dims, scale, reach, cuts=(), kind=jnp.bfloat16):
    values = scale * jax.random.normal(own_key, dims, jnp.float32)
    if cuts:
        values = values * steps_of(own_key, dims, cuts, -0.22, 0.18)
    return jnp.clip(values, -reach, reach).astype(kind)


def noise_with(own_key, extent, deviation, reach, pieces, heavy, kind=jnp.bfloat16):
    values = deviation * jax.random.normal(own_key, extent, jnp.float32)
    if pieces:
        values = values * steps_of(own_key, extent, pieces, -0.22, 0.18)
    return jnp.clip(with_spikes(values, jax.random.fold_in(own_key, 3), *heavy), -reach, reach).astype(kind)


def setup_inputs(seed: int = 0) -> dict:
    splits = jax.random.split(jax.random.key(seed), 6)
    features = scatter_about(splits[0], (3, KERNEL_FEATURES, TOKEN_COUNT), 1.0, 6.0, ((1, 16), (2, 64)))
    short_taps = scatter_about(splits[1], (3, TAPS, KERNEL_FEATURES), 0.6, 3.0, ((2, 16),), jnp.float32)
    long_filter = draw_long_filter(jax.random.fold_in(splits[5], 71), 0)
    skip_bias = jnp.clip(0.5 + 1.0 * jax.random.uniform(splits[3], (KERNEL_FEATURES,), jnp.float32) ** steps_of(splits[3], (KERNEL_FEATURES,), ((0, 16),), -0.2, 0.2), 0.5, 1.5)
    out_weight = noise_with(splits[4], (KERNEL_FEATURES, OUT_WIDTH), KERNEL_FEATURES ** -0.5, 0.125, ((0, 16),), (0, 1, 16, 2.0))
    return dict(features=features, short_taps=short_taps, long_filter=long_filter, skip_bias=skip_bias, out_weight=out_weight)


def block_conv(pair):
    product_block, filter_block = pair
    size = 2 * TOKEN_COUNT
    spectrum = jnp.fft.rfft(product_block, n=size, axis=-1) * jnp.fft.rfft(filter_block, n=size, axis=-1)
    return jnp.fft.irfft(spectrum, n=size, axis=-1)[:, :TOKEN_COUNT].astype(product_block.dtype)


def reference(features, short_taps, long_filter, skip_bias, out_weight):
    streams = features.astype(jnp.float32)
    padded = jnp.pad(streams, ((0, 0), (0, 0), (2, 0)))
    shaped = short_taps[:, 0, :, None] * streams + short_taps[:, 1, :, None] * padded[:, :, 1:-1] + short_taps[:, 2, :, None] * padded[:, :, :-2]
    gate = shaped[0].astype(jnp.bfloat16)
    kv_product = (shaped[1] * shaped[2]).astype(jnp.bfloat16)
    product_f = kv_product.astype(jnp.float32)
    filter_f = long_filter.astype(jnp.float32)
    blocks = KERNEL_FEATURES // 256
    long_part = lax.map(block_conv, (product_f.reshape(blocks, 256, TOKEN_COUNT), filter_f.reshape(blocks, 256, TOKEN_COUNT)))
    long_part = long_part.reshape(KERNEL_FEATURES, TOKEN_COUNT)
    mixed = lax.optimization_barrier((long_part + skip_bias[:, None] * product_f).astype(jnp.bfloat16))
    gated = (gate.astype(jnp.float32) * mixed.astype(jnp.float32)).astype(jnp.bfloat16)
    result = lax.dot_general(gated, out_weight, (((0,), (0,)), ((), ())), preferred_element_type=jnp.float32)
    return result.astype(jnp.bfloat16)
```

```python
import jax
import jax.numpy as jnp
from jax import lax
from jax.experimental import pallas as pl
from jax.experimental.pallas import tpu as pltpu
from jax.sharding import PartitionSpec as P

MESH = pl.DeviceIdType.MESH
F32 = jnp.float32
BF16 = jnp.bfloat16
SIDE = 256
LANES = 128
PARTS = 4
LAG = 4
STEPS = 7 * PARTS


def remote(src, dst, send_sem, recv_sem, device):
    return pltpu.make_async_remote_copy(
        src_ref=src, dst_ref=dst, send_sem=send_sem, recv_sem=recv_sem,
        device_id=device, device_id_type=MESH,
    )


def kernel(
    feat_hbm, taps_ref, filt_hbm, bias_ref, w_hbm, out_ref,
    feat, filt, w, cols, halo_out, halo_in, bias_in, gate, kv,
    filt_xy, filt_zs, filt_zr, kv_xy, kv_zs, kv_zr,
    mix_zs, mix_zr, mix_ss, mix,
    turn, hpad, xpad, ypad, piece, xs_buf, toep, gated_t,
    sib_out, sib_in, own, right_out, right_in, left_out, left_in,
    load_sem, halo_sem, bias_sem,
    xy_send, xy_recv, z_send, z_recv, back_send, back_recv,
    sib_send, sib_recv, right_send, right_recv, left_send, left_recv,
):
    context = lax.axis_index("context")
    tensor = lax.axis_index("tensor")
    here = (context // 16) * 4 + context % 4
    z_hi = (context // 4) % 4
    z_lo = tensor // 2
    core = tensor % 2

    def plane(place):
        return ((place // 4) * 16 + z_hi * 4 + place % 4, tensor)

    def across(target_hi):
        return (
            (context // 16) * 16 + target_hi * 4 + context % 4,
            ((z_lo + 4) % 8) * 2 + core,
        )

    after = ((context + 1) % 64, tensor)
    before = ((context + 63) % 64, tensor)
    sibling = (context, z_lo * 2 + 1 - core)
    right = (context, ((z_lo + 1) % 8) * 2 + core)
    left = (context, ((z_lo + 7) % 8) * 2 + core)

    loads = [
        pltpu.make_async_copy(feat_hbm, feat, load_sem.at[0]),
        pltpu.make_async_copy(filt_hbm, filt, load_sem.at[1]),
        pltpu.make_async_copy(w_hbm, w, load_sem.at[2]),
    ]
    for load in loads:
        load.start()

    barrier = pltpu.get_barrier_semaphore()
    peers = [plane((here + step) % 16) for step in range(1, 16)]
    peers += [across((z_hi + step) % 4) for step in range(4)]
    peers += [before, sibling, right, left]
    for peer in peers:
        pl.semaphore_signal(barrier, inc=1, device_id=peer, device_id_type=MESH)

    loads[0].wait()
    loads[1].wait()

    row = lax.broadcasted_iota(jnp.int32, (16, SIDE), 0)
    pos = lax.broadcasted_iota(jnp.int32, (16, SIDE), 1)
    edge = jnp.zeros((16, SIDE), F32)
    for stream in range(3):
        pick = ((row - 2 * stream == pos - (SIDE - 2)) & (pos >= SIDE - 2)).astype(F32).astype(BF16)
        edge = edge + lax.dot_general(
            pick, feat[stream], (((1,), (1,)), ((), ())), preferred_element_type=F32
        )
    halo_out[...] = edge.astype(BF16)
    cols[...] = jnp.zeros((LANES, SIDE), F32)
    for stream in range(3):
        for tap in range(3):
            cols[pl.ds(3 * stream + tap, 1), :] = taps_ref[stream, pl.ds(tap, 1), :]
    hpad[:, 0:8, :] = jnp.zeros((4, 8, LANES), F32)
    xpad[:, 0:16, :] = jnp.zeros((4, 16, LANES), F32)

    pl.semaphore_wait(barrier, len(peers))

    halo_copy = remote(halo_out, halo_in, halo_sem.at[0], halo_sem.at[1], after)
    halo_copy.start()
    bias_copy = remote(bias_ref, bias_in, bias_sem.at[0], bias_sem.at[1], across(z_hi))
    bias_copy.start()

    sent = [halo_copy, bias_copy]

    def plane_exchange(src, dst, which):
        copies = []
        for step in range(1, 16):
            to = (here + step) % 16
            copy = remote(
                src.at[pl.ds(pl.multiple_of(to * 16, 16), 16)],
                dst.at[pl.ds(pl.multiple_of(here * 16, 16), 16)],
                xy_send.at[which, step], xy_recv.at[which, step], plane(to),
            )
            copy.start()
            copies.append(copy)
        mine = pl.ds(pl.multiple_of(here * 16, 16), 16)
        dst[mine, :] = src[mine, :]
        sent.extend(copies)
        return copies

    def across_exchange(src, dst, which):
        copies = []
        for step in (2, 1, 3, 0):
            to = (z_hi + step) % 4
            copy = remote(
                src.at[pl.ds(pl.multiple_of(to * 64, 64), 64)],
                dst.at[pl.ds(pl.multiple_of(z_hi * 64, 64), 64)],
                z_send.at[which, step], z_recv.at[which, step], across(to),
            )
            copy.start()
            copies.append(copy)
        sent.extend(copies)
        return copies

    def arrived(copies):
        for copy in copies:
            copy.wait_recv()

    def swap_blocks(src, dst):
        for half in range(2):
            lanes = pl.ds(half * LANES, LANES)
            turn[half] = src[:, lanes].astype(F32)
        for j in range(16):
            for half in range(2):
                block = turn[half, pl.ds(j, 16, stride=16), :]
                dst[pl.ds(16 * j, 16), pl.ds(half * LANES, LANES)] = block.astype(BF16)

    def spread(src, dst, ahead):
        for zs in range(4):
            for ch in range(4):
                tile = src[pl.ds(zs * 64 + ch * 16, 16), :].astype(F32)
                for xs in range(4):
                    for half in range(2):
                        first = ahead + (xs * 16 + zs * 4) * 2 + half
                        dst[ch, pl.ds(first, 4, stride=2), :] = tile[
                            4 * xs : 4 * xs + 4, half * LANES : (half + 1) * LANES
                        ]

    filt_plane = plane_exchange(filt, filt_xy, 0)
    arrived(filt_plane)
    swap_blocks(filt_xy, filt_zs)
    filt_across = across_exchange(filt_zs, filt_zr, 0)

    halo_copy.wait_recv()
    seen = jnp.where(context > 0, 1.0, 0.0)
    cols[16:32, :] = halo_in[...].astype(F32) * seen
    turned = cols[...].T
    lane = lax.broadcasted_iota(jnp.int32, (64, SIDE), 1)
    for block in range(4):
        rows = slice(64 * block, 64 * block + 64)
        shaped = []
        for stream in range(3):
            now = feat[stream, rows, :].astype(F32)
            last = turned[rows, 16 + 2 * stream + 1 : 16 + 2 * stream + 2]
            older = turned[rows, 16 + 2 * stream : 16 + 2 * stream + 1]
            one = jnp.where(lane == 0, last, pltpu.roll(now, 1, 1))
            two = jnp.where(lane == 0, older, jnp.where(lane == 1, last, pltpu.roll(now, 2, 1)))
            tap = [turned[rows, 3 * stream + j : 3 * stream + j + 1] for j in range(3)]
            shaped.append(tap[0] * now + tap[1] * one + tap[2] * two)
        gate[rows, :] = shaped[0].astype(BF16)
        kv[rows, :] = (shaped[1] * shaped[2]).astype(BF16)

    kv_plane = plane_exchange(kv, kv_xy, 1)
    arrived(kv_plane)
    swap_blocks(kv_xy, kv_zs)
    kv_across = across_exchange(kv_zs, kv_zr, 1)

    arrived(filt_across)
    spread(filt_zr, hpad, 8)

    lower = lax.broadcasted_iota(jnp.int32, (LANES, LANES), 1)
    upper = lax.broadcasted_iota(jnp.int32, (LANES, LANES), 0)
    keep = lower + upper < LANES

    def build(index, carry):
        ch = index // 16
        b = index % 16
        for a in range(8):
            now = hpad[ch, pl.ds(8 + 16 * a + b, 1), :]
            past = hpad[ch, pl.ds(7 + 16 * a + b, 1), :]
            block = jnp.where(
                keep,
                jnp.broadcast_to(now, (LANES, LANES)),
                jnp.broadcast_to(past, (LANES, LANES)),
            )
            block = pltpu.roll(block, 0, 1, stride=1, stride_axis=0)
            toep[ch, pl.ds(pl.multiple_of(b * LANES, LANES), LANES), pl.ds(a * LANES, LANES)] = (
                block.astype(BF16)
            )
        return carry

    lax.fori_loop(0, 64, build, 0)

    bias_copy.wait_recv()
    arrived(kv_across)
    spread(kv_zr, xpad, 16)

    back = []
    for ch in range(4):
        for b in range(16):
            xs_buf[:, pl.ds(b * LANES, LANES)] = xpad[ch, pl.ds(16 - b, LANES), :].astype(BF16)
        total = None
        for a in range(4):
            part = jnp.dot(
                xs_buf[pl.ds(0, LANES - 32 * a), :],
                toep[ch, :, pl.ds(2 * a * LANES, 2 * LANES)],
                preferred_element_type=F32,
            )
            low, high = part[:, :LANES], part[: LANES - 32 * a - 16, LANES:]
            if a:
                low = jnp.concatenate([jnp.zeros((32 * a, LANES), F32), low], axis=0)
            high = jnp.concatenate([jnp.zeros((32 * a + 16, LANES), F32), high], axis=0)
            total = low + high if total is None else total + low + high
        channel = here * 16 + z_hi * 4 + ch
        spot = lax.broadcasted_iota(jnp.int32, (1, SIDE), 1)
        bias = jnp.sum(jnp.where(spot == channel, bias_in[...], 0.0), axis=1, keepdims=True)
        ypad[...] = total + bias * xpad[ch, pl.ds(16, LANES), :]
        for zs in range(4):
            for xs in range(4):
                for half in range(2):
                    first = (xs * 16 + zs * 4) * 2 + half
                    piece[pl.ds(4 * xs, 4), pl.ds(half * LANES, LANES)] = ypad[
                        pl.ds(first, 4, stride=2), :
                    ]
            mix_zs[pl.ds(zs * 64 + ch * 16, 16), :] = piece[...].astype(BF16)
        for step in (2, 1, 3, 0):
            to = (z_hi + step) % 4
            copy = remote(
                mix_zs.at[pl.ds(pl.multiple_of(to * 64 + ch * 16, 16), 16)],
                mix_zr.at[pl.ds(pl.multiple_of(z_hi * 64 + ch * 16, 16), 16)],
                back_send.at[ch, step], back_recv.at[ch, step], across(to),
            )
            copy.start()
            back.append(copy)
    sent.extend(back)

    arrived(back)
    swap_blocks(mix_zr, mix_ss)
    arrived(plane_exchange(mix_ss, mix, 2))

    gated = (gate[...].astype(F32) * mix[...].astype(F32)).astype(BF16).astype(F32)
    gated_t[...] = gated.T.astype(BF16)
    loads[2].wait()

    def sib_copy(d):
        return remote(sib_out.at[d], sib_in.at[d], sib_send.at[d], sib_recv.at[d], sibling)

    for d in (7, 0, 6, 1, 5, 2, 4, 3):
        theirs = pl.ds(pl.multiple_of((2 * d + 1 - core) * SIDE, SIDE), SIDE)
        mine = pl.ds(pl.multiple_of((2 * d + core) * SIDE, SIDE), SIDE)
        sib_out[d] = jnp.dot(gated_t[...], w[:, theirs], preferred_element_type=F32).astype(BF16)
        sib_copy(d).start()
        own[d] = jnp.dot(gated_t[...], w[:, mine], preferred_element_type=F32)

    size = SIDE // PARTS

    def rows_of(n):
        return pl.ds(pl.multiple_of((n % PARTS) * size, size), size)

    def right_copy(n):
        d = 7 - n // PARTS
        return remote(
            right_out.at[d, rows_of(n)], right_in.at[d, rows_of(n)],
            right_send.at[n], right_recv.at[n], right,
        )

    def left_copy(n):
        d = n // PARTS
        return remote(
            left_out.at[d, rows_of(n)], left_in.at[d, rows_of(n)],
            left_send.at[n], left_recv.at[n], left,
        )

    def pass_on(n, d, first, copy, came, going):
        rows = rows_of(n)

        @pl.when(n % PARTS == 0)
        def _():
            sib_copy(d).wait_recv()

        @pl.when(first)
        def _():
            going[d, rows, :] = (own[d, rows, :] + sib_in[d, rows, :].astype(F32)).astype(BF16)

        @pl.when(jnp.logical_not(first))
        def _():
            copy.wait_recv()
            going[d, rows, :] = (
                own[d, rows, :] + sib_in[d, rows, :].astype(F32) + came[d, rows, :].astype(F32)
            ).astype(BF16)

        copy.start()

    def reduce_step(moment, carry):
        n = moment - z_lo * LAG

        @pl.when((n >= 0) & (n < (7 - z_lo) * PARTS))
        def _():
            pass_on(n, 7 - n // PARTS, z_lo == 0, right_copy(n), right_in, right_out)

        m = moment - (7 - z_lo) * LAG

        @pl.when((m >= 0) & (m < z_lo * PARTS))
        def _():
            pass_on(m, m // PARTS, z_lo == 7, left_copy(m), left_in, left_out)

        return carry

    lax.fori_loop(0, STEPS + 6 * LAG, reduce_step, 0)

    sib_copy(z_lo).wait_recv()
    own[z_lo] = own[z_lo] + sib_in[z_lo].astype(F32)

    @pl.when(z_lo > 0)
    def _():
        for part in range(PARTS):
            n = (7 - z_lo) * PARTS + part
            right_copy(n).wait_recv()
        own[z_lo] = own[z_lo] + right_in[z_lo].astype(F32)

    @pl.when(z_lo < 7)
    def _():
        for part in range(PARTS):
            n = z_lo * PARTS + part
            left_copy(n).wait_recv()
        own[z_lo] = own[z_lo] + left_in[z_lo].astype(F32)

    out_ref[...] = own[z_lo].astype(BF16)

    for copy in sent:
        copy.wait_send()
    for d in range(8):
        sib_copy(d).wait_send()

    def close(n, carry):
        @pl.when(n < (7 - z_lo) * PARTS)
        def _():
            right_copy(n).wait_send()

        @pl.when(n < z_lo * PARTS)
        def _():
            left_copy(n).wait_send()

        return carry

    lax.fori_loop(0, STEPS, close, 0)


def local(features, short_taps, long_filter, skip_bias, out_weight):
    vmem = pl.BlockSpec(memory_space=pltpu.VMEM)
    anywhere = pl.BlockSpec(memory_space=pl.ANY)
    square = pltpu.VMEM((SIDE, SIDE), BF16)
    dma = pltpu.SemaphoreType.DMA
    return pl.pallas_call(
        kernel,
        out_shape=jax.ShapeDtypeStruct((SIDE, SIDE), BF16),
        in_specs=[anywhere, vmem, anywhere, vmem, anywhere],
        out_specs=vmem,
        scratch_shapes=[
            pltpu.VMEM((3, SIDE, SIDE), BF16),
            square,
            pltpu.VMEM((SIDE, 16 * SIDE), BF16),
            pltpu.VMEM((LANES, SIDE), F32),
            pltpu.VMEM((16, SIDE), BF16),
            pltpu.VMEM((16, SIDE), BF16),
            pltpu.VMEM((1, SIDE), F32),
            square, square,
            square, square, square,
            square, square, square,
            square, square, square, square,
            pltpu.VMEM((2, SIDE, LANES), F32),
            pltpu.VMEM((4, 136, LANES), F32),
            pltpu.VMEM((4, 144, LANES), F32),
            pltpu.VMEM((LANES, LANES), F32),
            pltpu.VMEM((16, SIDE), F32),
            pltpu.VMEM((LANES, 2048), BF16),
            pltpu.VMEM((4, 2048, 1024), BF16),
            square,
            pltpu.VMEM((8, SIDE, SIDE), BF16),
            pltpu.VMEM((8, SIDE, SIDE), BF16),
            pltpu.VMEM((8, SIDE, SIDE), F32),
            pltpu.VMEM((8, SIDE, SIDE), BF16),
            pltpu.VMEM((8, SIDE, SIDE), BF16),
            pltpu.VMEM((8, SIDE, SIDE), BF16),
            pltpu.VMEM((8, SIDE, SIDE), BF16),
            dma((3,)), dma((2,)), dma((2,)),
            dma((3, 16)), dma((3, 16)),
            dma((2, 4)), dma((2, 4)),
            dma((4, 4)), dma((4, 4)),
            dma((8,)), dma((8,)),
            dma((STEPS,)), dma((STEPS,)), dma((STEPS,)), dma((STEPS,)),
        ],
        compiler_params=pltpu.CompilerParams(
            collective_id=0, has_side_effects=True, vmem_limit_bytes=50 << 20
        ),
        cost_estimate=pl.CostEstimate(
            flops=4 * 10**9, bytes_accessed=3 * 10**6, transcendentals=0
        ),
        name="hyena_operator",
    )(features, short_taps, long_filter, skip_bias.reshape(1, SIDE), out_weight)


def solution(mesh):
    placed = (
        P(None, "tensor", "context"),
        P(None, None, "tensor"),
        P("tensor", "context"),
        P("tensor"),
        P("tensor", None),
    )
    return jax.shard_map(
        local, mesh=mesh, in_specs=placed, out_specs=P("context", "tensor"), check_vma=False
    )
```

```python
import jax
import jax.numpy as jnp
from jax import lax
from jax.experimental import pallas as pl
from jax.experimental.pallas import tpu as pltpu
from jax.sharding import PartitionSpec as P

MESH = pl.DeviceIdType.MESH
F32 = jnp.float32
BF16 = jnp.bfloat16
SIDE = 256
LANES = 128
PARTS = 4
LAG = 4
STEPS = 7 * PARTS


def remote(src, dst, send_sem, recv_sem, device):
    return pltpu.make_async_remote_copy(
        src_ref=src, dst_ref=dst, send_sem=send_sem, recv_sem=recv_sem,
        device_id=device, device_id_type=MESH,
    )


def kernel(
    feat_hbm, taps_hbm, filt_hbm, bias_hbm, w_hbm, out_ref,
    feat, taps, filt, bias_out, w, cols, halo_out, halo_in, bias_in, gate, kv,
    filt_pre, filt_zr, filt_zs, filt_xy, filt_all, kv_xy, kv_zs, kv_zr,
    mix_zs, mix_zr, mix_ss, mix,
    turn, hpad, ahead, behind, xpad, pairs, sums, folded, ypad, piece, xs_buf, toep, gated_t,
    sib_out, sib_in, own, right_out, right_in, right_far, left_out, left_in, left_far,
    load_sem, halo_sem, bias_sem,
    xy_send, xy_recv, z_send, z_recv, kv_send, kv_recv, back_send, back_recv,
    sib_send, sib_recv, right_send, right_recv, left_send, left_recv,
):
    context = lax.axis_index("context")
    tensor = lax.axis_index("tensor")
    x = lax.div(context, 16)
    y = lax.rem(context, 4)
    z_hi = lax.rem(lax.div(context, 4), 4)
    z_lo = lax.div(tensor, 2)
    core = lax.rem(tensor, 2)
    here = x * 4 + y

    def plane(step):
        to_x = lax.rem(x + step // 4, 4)
        to_y = lax.rem(y + step % 4, 4)
        return to_x * 4 + to_y, (to_x * 16 + z_hi * 4 + to_y, tensor)

    opposite = lax.rem(z_lo + 4, 8) * 2 + core

    def across(target_hi):
        return (x * 16 + target_hi * 4 + y, opposite)

    def along(target_lo):
        return (context, target_lo * 2 + core)

    after = (lax.rem(context + 1, 64), tensor)
    before = (lax.rem(context + 63, 64), tensor)
    sibling = (context, z_lo * 2 + 1 - core)
    right = along(lax.rem(z_lo + 1, 8))
    left = along(lax.rem(z_lo + 7, 8))

    def swap_blocks(src, dst):
        for half in range(2):
            lanes = pl.ds(half * LANES, LANES)
            turn[half] = src[:, lanes].astype(F32)
        for j in range(16):
            for half in range(2):
                block = turn[half, pl.ds(j, 16, stride=16), :]
                dst[pl.ds(16 * j, 16), pl.ds(half * LANES, LANES)] = block.astype(BF16)

    loads = [
        pltpu.make_async_copy(feat_hbm, feat, load_sem.at[0]),
        pltpu.make_async_copy(filt_hbm, filt, load_sem.at[1]),
        pltpu.make_async_copy(w_hbm, w, load_sem.at[2]),
        pltpu.make_async_copy(taps_hbm, taps, load_sem.at[3]),
        pltpu.make_async_copy(bias_hbm, bias_out, load_sem.at[4]),
    ]
    for which in (1, 0, 3, 4, 2):
        loads[which].start()

    barrier = pltpu.get_barrier_semaphore()
    peers = [across(lax.rem(z_hi + step, 4)) for step in (2, 1, 3, 0)]
    peers += [before]
    peers += [along(lax.rem(z_lo + step, 8)) for step in range(1, 8)]
    peers += [plane(step)[1] for step in range(1, 16)]
    peers += [sibling]
    for peer in peers:
        pl.semaphore_signal(barrier, inc=1, device_id=peer, device_id_type=MESH)

    loads[1].wait()
    swap_blocks(filt, filt_pre)
    for which in (0, 3, 4):
        loads[which].wait()

    row = lax.broadcasted_iota(jnp.int32, (16, SIDE), 0)
    pos = lax.broadcasted_iota(jnp.int32, (16, SIDE), 1)
    edge = jnp.zeros((16, SIDE), F32)
    for stream in range(3):
        pick = ((row - 2 * stream == pos - (SIDE - 2)) & (pos >= SIDE - 2)).astype(F32).astype(BF16)
        edge = edge + lax.dot_general(
            pick, feat[stream], (((1,), (1,)), ((), ())), preferred_element_type=F32
        )
    halo_out[...] = edge.astype(BF16)
    cols[...] = jnp.zeros((LANES, SIDE), F32)
    for stream in range(3):
        for tap in range(3):
            cols[pl.ds(3 * stream + tap, 1), :] = taps[stream, pl.ds(tap, 1), :]
    hpad[:, 0:8, :] = jnp.zeros((4, 8, LANES), F32)
    xpad[:, 0:8, :] = jnp.zeros((4, 8, LANES), F32)
    pairs[0:32, :] = jnp.zeros((32, LANES), F32)
    sums[0:32, :] = jnp.zeros((32, LANES), F32)

    pl.semaphore_wait(barrier, len(peers))

    sent = []
    halo_copy = remote(halo_out, halo_in, halo_sem.at[0], halo_sem.at[1], after)
    halo_copy.start()
    bias_copy = remote(bias_out, bias_in, bias_sem.at[0], bias_sem.at[1], across(z_hi))
    bias_copy.start()

    sent.extend([halo_copy, bias_copy])

    def plane_exchange(src, dst, which):
        copies = []
        for step in range(1, 16):
            to, device = plane(step)
            copy = remote(
                src.at[pl.ds(pl.multiple_of(to * 16, 16), 16)],
                dst.at[pl.ds(pl.multiple_of(here * 16, 16), 16)],
                xy_send.at[which, step], xy_recv.at[which, step], device,
            )
            copy.start()
            copies.append(copy)
        mine = pl.ds(pl.multiple_of(here * 16, 16), 16)
        dst[mine, :] = src[mine, :]
        sent.extend(copies)
        return copies

    def across_exchange(src, dst, send, recv, first, rows):
        copies = []
        for step in (2, 1, 3, 0):
            to = lax.rem(z_hi + step, 4)
            copy = remote(
                src.at[pl.ds(pl.multiple_of(to * 64 + first, 16), rows)],
                dst.at[pl.ds(pl.multiple_of(z_hi * 64 + first, 16), rows)],
                send.at[step], recv.at[step], across(to),
            )
            copy.start()
            copies.append(copy)
        sent.extend(copies)
        return copies

    def arrived(copies):
        for copy in copies:
            copy.wait_recv()

    def spread(src, dst, start, ch):
        for zs in range(4):
            tile = src[pl.ds(zs * 64 + ch * 16, 16), :].astype(F32)
            for xs in range(4):
                for half in range(2):
                    first = start + (xs * 16 + zs * 4) * 2 + half
                    dst[ch, pl.ds(first, 4, stride=2), :] = tile[
                        4 * xs : 4 * xs + 4, half * LANES : (half + 1) * LANES
                    ]

    filt_across = across_exchange(filt_pre, filt_zr, z_send, z_recv, 0, 64)

    halo_copy.wait_recv()
    seen = jnp.where(context > 0, 1.0, 0.0)
    cols[16:32, :] = halo_in[...].astype(F32) * seen
    turned = cols[...].T
    lane = lax.broadcasted_iota(jnp.int32, (64, SIDE), 1)
    for block in range(4):
        rows = slice(64 * block, 64 * block + 64)
        shaped = []
        for stream in range(3):
            now = feat[stream, rows, :].astype(F32)
            last = turned[rows, 16 + 2 * stream + 1 : 16 + 2 * stream + 2]
            older = turned[rows, 16 + 2 * stream : 16 + 2 * stream + 1]
            one = jnp.where(lane == 0, last, pltpu.roll(now, 1, 1))
            two = jnp.where(lane == 0, older, jnp.where(lane == 1, last, pltpu.roll(now, 2, 1)))
            tap = [turned[rows, 3 * stream + j : 3 * stream + j + 1] for j in range(3)]
            shaped.append(tap[0] * now + tap[1] * one + tap[2] * two)
        gate[rows, :] = shaped[0].astype(BF16)
        kv[rows, :] = (shaped[1] * shaped[2]).astype(BF16)

    kv_plane = plane_exchange(kv, kv_xy, 1)
    arrived(kv_plane)
    swap_blocks(kv_xy, kv_zs)
    kv_across = [
        across_exchange(kv_zs, kv_zr, kv_send.at[ch], kv_recv.at[ch], 16 * ch, 16)
        for ch in range(4)
    ]

    arrived(filt_across)
    swap_blocks(filt_zr, filt_zs)
    arrived(plane_exchange(filt_zs, filt_xy, 0))
    swap_blocks(filt_xy, filt_all)
    for ch in range(4):
        spread(filt_all, hpad, 8, ch)

    low = lax.broadcasted_iota(jnp.int32, (16, LANES), 1) < 64
    for ch in range(4):
        for a in range(4):
            one = hpad[ch, pl.ds(8 + 32 * a, 16), :]
            two = hpad[ch, pl.ds(24 + 32 * a, 16), :]
            even = jnp.where(low, one, pltpu.roll(two, 64, 1))
            odd = jnp.where(low, pltpu.roll(one, 64, 1), two)
            ahead[ch, pl.ds(32 * a, 16, stride=2), :] = even
            ahead[ch, pl.ds(32 * a + 1, 16, stride=2), :] = odd
            behind[ch, pl.ds(32 * a + 1, 16, stride=2), :] = pltpu.roll(even, 64, 1)
            behind[ch, pl.ds(32 * a + 2, 16, stride=2), :] = pltpu.roll(odd, 64, 1)
        for a in range(4):
            one = hpad[ch, pl.ds(23 + 32 * a, 1), :]
            two = hpad[ch, pl.ds(7 + 32 * a, 1), :]
            behind[ch, pl.ds(32 * a, 1), :] = jnp.where(low[:1], pltpu.roll(one, 64, 1), two)
    lane = lax.broadcasted_iota(jnp.int32, (64, LANES), 1)
    down = lax.broadcasted_iota(jnp.int32, (64, LANES), 0)
    keep = lax.rem(lane, 64) + down < 64

    def build(index, carry):
        ch = lax.div(index, 32)
        b = lax.rem(index, 32)
        for a in range(4):
            block = jnp.where(
                keep,
                jnp.broadcast_to(ahead[ch, pl.ds(32 * a + b, 1), :], (64, LANES)),
                jnp.broadcast_to(behind[ch, pl.ds(32 * a + b, 1), :], (64, LANES)),
            )
            block = pltpu.roll(block, 0, 1, stride=1, stride_axis=0)
            toep[ch, pl.ds(pl.multiple_of(b * 64, 64), 64), pl.ds(a * LANES, LANES)] = (
                block.astype(BF16)
            )
        return carry

    lax.fori_loop(0, 128, build, 0)

    bias_copy.wait_recv()
    spot = lax.broadcasted_iota(jnp.int32, (1, SIDE), 1)
    first_lanes = lax.broadcasted_iota(jnp.int32, (LANES, LANES), 1) < 64
    back = []
    for ch in range(4):
        arrived(kv_across[ch])
        spread(kv_zr, xpad, 8, ch)
        own_row = xpad[ch, pl.ds(8, LANES), :]
        row_before = xpad[ch, pl.ds(7, LANES), :]
        pairs[pl.ds(32, LANES, stride=2), :] = jnp.where(first_lanes, own_row, row_before)
        pairs[pl.ds(33, LANES, stride=2), :] = pltpu.roll(own_row, 64, 1)
        for b in range(16):
            xs_buf[:, pl.ds(b * LANES, LANES)] = pairs[pl.ds(32 - 2 * b, SIDE), :].astype(BF16)
        upper = jnp.dot(xs_buf[...], toep[ch, :, pl.ds(0, SIDE)], preferred_element_type=F32)
        lower = jnp.dot(
            xs_buf[pl.ds(0, LANES), :], toep[ch, :, pl.ds(SIDE, SIDE)],
            preferred_element_type=F32,
        )
        sums[pl.ds(32, SIDE), :] = upper[:, :LANES]
        sums[pl.ds(96, 192), :] += upper[:192, LANES:]
        sums[pl.ds(160, LANES), :] += lower[:, :LANES]
        sums[pl.ds(224, 64), :] += lower[:64, LANES:]
        folded[...] = sums[pl.ds(32, SIDE), :] + pltpu.roll(sums[pl.ds(0, SIDE), :], 64, 1)
        total = jnp.where(
            first_lanes,
            folded[pl.ds(0, LANES, stride=2), :],
            pltpu.roll(folded[pl.ds(1, LANES, stride=2), :], 64, 1),
        )
        channel = here * 16 + z_hi * 4 + ch
        bias = jnp.sum(jnp.where(spot == channel, bias_in[...], 0.0), axis=1, keepdims=True)
        ypad[...] = total + bias * own_row
        for zs in range(4):
            for xs in range(4):
                for half in range(2):
                    first = (xs * 16 + zs * 4) * 2 + half
                    piece[pl.ds(4 * xs, 4), pl.ds(half * LANES, LANES)] = ypad[
                        pl.ds(first, 4, stride=2), :
                    ]
            mix_zs[pl.ds(zs * 64 + ch * 16, 16), :] = piece[...].astype(BF16)
        back += across_exchange(
            mix_zs, mix_zr, back_send.at[ch], back_recv.at[ch], 16 * ch, 16
        )

    arrived(back)
    swap_blocks(mix_zr, mix_ss)
    arrived(plane_exchange(mix_ss, mix, 2))

    gated = (gate[...].astype(F32) * mix[...].astype(F32)).astype(BF16).astype(F32)
    gated_t[...] = gated.T.astype(BF16)
    loads[2].wait()

    def sib_copy(d):
        return remote(sib_out.at[d], sib_in.at[d], sib_send.at[d], sib_recv.at[d], sibling)

    for d in (7, 0, 6, 1, 5, 2, 4, 3):
        theirs = pl.ds(pl.multiple_of((2 * d + 1 - core) * SIDE, SIDE), SIDE)
        mine = pl.ds(pl.multiple_of((2 * d + core) * SIDE, SIDE), SIDE)
        sib_out[d] = jnp.dot(gated_t[...], w[:, theirs], preferred_element_type=F32).astype(BF16)
        sib_copy(d).start()
        own[d] = jnp.dot(gated_t[...], w[:, mine], preferred_element_type=F32)

    size = SIDE // PARTS

    def rows_of(n):
        return pl.ds(pl.multiple_of(lax.rem(n, PARTS) * size, size), size)

    quarter = lax.rem(z_lo, 4)

    def right_copy(n):
        d = 7 - lax.div(n, PARTS)
        return remote(
            right_out.at[d, rows_of(n)], right_in.at[d, rows_of(n)],
            right_send.at[n], right_recv.at[n], right,
        )

    def right_jump(n, d):
        return remote(
            right_out.at[7 - lax.div(n, PARTS), rows_of(n)], right_far.at[rows_of(n)],
            right_send.at[n], right_recv.at[STEPS + lax.rem(n, PARTS)], along(d),
        )

    def left_copy(n):
        d = lax.div(n, PARTS)
        return remote(
            left_out.at[d, rows_of(n)], left_in.at[d, rows_of(n)],
            left_send.at[n], left_recv.at[n], left,
        )

    def left_jump(n, d):
        return remote(
            left_out.at[lax.div(n, PARTS), rows_of(n)], left_far.at[rows_of(n)],
            left_send.at[n], left_recv.at[STEPS + lax.rem(n, PARTS)], along(d),
        )

    def pass_on(n, d, first, jumps, copy, jump, came, going):
        rows = rows_of(n)

        @pl.when(lax.rem(n, PARTS) == 0)
        def _():
            sib_copy(d).wait_recv()

        @pl.when(first)
        def _():
            going[d, rows, :] = (own[d, rows, :] + sib_in[d, rows, :].astype(F32)).astype(BF16)

        @pl.when(jnp.logical_not(first))
        def _():
            copy.wait_recv()
            going[d, rows, :] = (
                own[d, rows, :] + sib_in[d, rows, :].astype(F32) + came[d, rows, :].astype(F32)
            ).astype(BF16)

        @pl.when(jumps)
        def _():
            jump.start()

        @pl.when(jnp.logical_not(jumps))
        def _():
            copy.start()

    def reduce_step(moment, carry):
        n = moment - quarter * LAG

        @pl.when((n >= 0) & (n < (7 - z_lo) * PARTS))
        def _():
            d = 7 - lax.div(n, PARTS)
            pass_on(
                n, d, quarter == 0, (z_lo == 3) & (d > 4),
                right_copy(n), right_jump(n, d), right_in, right_out,
            )

        m = moment - (3 - quarter) * LAG

        @pl.when((m >= 0) & (m < z_lo * PARTS))
        def _():
            d = lax.div(m, PARTS)
            pass_on(
                m, d, quarter == 3, (z_lo == 4) & (d < 3),
                left_copy(m), left_jump(m, d), left_in, left_out,
            )

        return carry

    lax.fori_loop(0, STEPS + 3 * LAG, reduce_step, 0)

    sib_copy(z_lo).wait_recv()
    own[z_lo] = own[z_lo] + sib_in[z_lo].astype(F32)

    @pl.when(z_lo > 0)
    def _():
        for part in range(PARTS):
            right_copy((7 - z_lo) * PARTS + part).wait_recv()
        own[z_lo] = own[z_lo] + right_in[z_lo].astype(F32)

    @pl.when(z_lo < 7)
    def _():
        for part in range(PARTS):
            left_copy(z_lo * PARTS + part).wait_recv()
        own[z_lo] = own[z_lo] + left_in[z_lo].astype(F32)

    @pl.when(z_lo > 4)
    def _():
        for part in range(PARTS):
            right_jump(part, z_lo).wait_recv()
        own[z_lo] = own[z_lo] + right_far[...].astype(F32)

    @pl.when(z_lo < 3)
    def _():
        for part in range(PARTS):
            left_jump(part, z_lo).wait_recv()
        own[z_lo] = own[z_lo] + left_far[...].astype(F32)

    out_ref[...] = own[z_lo].astype(BF16)

    for copy in sent:
        copy.wait_send()
    for d in range(8):
        sib_copy(d).wait_send()

    def close(n, carry):
        @pl.when(n < (7 - z_lo) * PARTS)
        def _():
            right_copy(n).wait_send()

        @pl.when(n < z_lo * PARTS)
        def _():
            left_copy(n).wait_send()

        return carry

    lax.fori_loop(0, STEPS, close, 0)


def local(features, short_taps, long_filter, skip_bias, out_weight):
    vmem = pl.BlockSpec(memory_space=pltpu.VMEM)
    anywhere = pl.BlockSpec(memory_space=pl.ANY)
    square = pltpu.VMEM((SIDE, SIDE), BF16)
    dma = pltpu.SemaphoreType.DMA
    return pl.pallas_call(
        kernel,
        out_shape=jax.ShapeDtypeStruct((SIDE, SIDE), BF16),
        in_specs=[anywhere] * 5,
        out_specs=vmem,
        scratch_shapes=[
            pltpu.VMEM((3, SIDE, SIDE), BF16),
            pltpu.VMEM((3, 3, SIDE), F32),
            square,
            pltpu.VMEM((1, SIDE), F32),
            pltpu.VMEM((SIDE, 16 * SIDE), BF16),
            pltpu.VMEM((LANES, SIDE), F32),
            pltpu.VMEM((16, SIDE), BF16),
            pltpu.VMEM((16, SIDE), BF16),
            pltpu.VMEM((1, SIDE), F32),
            square, square,
            square, square, square, square, square,
            square, square, square,
            square, square, square, square,
            pltpu.VMEM((2, SIDE, LANES), F32),
            pltpu.VMEM((4, 136, LANES), F32),
            pltpu.VMEM((4, LANES, LANES), F32),
            pltpu.VMEM((4, 136, LANES), F32),
            pltpu.VMEM((4, 136, LANES), F32),
            pltpu.VMEM((32 + SIDE, LANES), F32),
            pltpu.VMEM((32 + SIDE, LANES), F32),
            pltpu.VMEM((SIDE, LANES), F32),
            pltpu.VMEM((LANES, LANES), F32),
            pltpu.VMEM((16, SIDE), F32),
            pltpu.VMEM((SIDE, 2048), BF16),
            pltpu.VMEM((4, 2048, 512), BF16),
            square,
            pltpu.VMEM((8, SIDE, SIDE), BF16),
            pltpu.VMEM((8, SIDE, SIDE), BF16),
            pltpu.VMEM((8, SIDE, SIDE), F32),
            pltpu.VMEM((8, SIDE, SIDE), BF16), pltpu.VMEM((8, SIDE, SIDE), BF16), square,
            pltpu.VMEM((8, SIDE, SIDE), BF16), pltpu.VMEM((8, SIDE, SIDE), BF16), square,
            dma((5,)), dma((2,)), dma((2,)),
            dma((3, 16)), dma((3, 16)),
            dma((4,)), dma((4,)),
            dma((4, 4)), dma((4, 4)),
            dma((4, 4)), dma((4, 4)),
            dma((8,)), dma((8,)),
            dma((STEPS,)), dma((STEPS + PARTS,)), dma((STEPS,)), dma((STEPS + PARTS,)),
        ],
        compiler_params=pltpu.CompilerParams(
            collective_id=0, has_side_effects=True, vmem_limit_bytes=60 << 20
        ),
        cost_estimate=pl.CostEstimate(
            flops=4 * 10**9, bytes_accessed=3 * 10**6, transcendentals=0
        ),
        name="hyena_operator",
    )(features, short_taps, long_filter, skip_bias.reshape(1, SIDE), out_weight)


def solution(mesh):
    placed = (
        P(None, "tensor", "context"),
        P(None, None, "tensor"),
        P("tensor", "context"),
        P("tensor"),
        P("tensor", None),
    )
    return jax.shard_map(
        local, mesh=mesh, in_specs=placed, out_specs=P("context", "tensor"), check_vma=False
    )
```

```python
import jax
import jax.numpy as jnp
from jax import lax
from jax.experimental import pallas as pl
from jax.experimental.pallas import tpu as pltpu
from jax.sharding import PartitionSpec as P

MESH = pl.DeviceIdType.MESH
F32 = jnp.float32
BF16 = jnp.bfloat16
SIDE = 256
LANES = 128
PARTS = 2
LAG = 4
STEPS = 7 * PARTS


def remote(src, dst, send_sem, recv_sem, device):
    return pltpu.make_async_remote_copy(
        src_ref=src, dst_ref=dst, send_sem=send_sem, recv_sem=recv_sem,
        device_id=device, device_id_type=MESH,
    )


def kernel(
    feat_hbm, taps_hbm, filt_hbm, bias_hbm, w_hbm, out_ref,
    feat, taps, filt, bias_out, w, cols, halo_out, halo_in, bias_in, gate, kv,
    filt_pre, filt_zr, filt_zs, filt_xy, filt_all, kv_xy, kv_zs, kv_zr,
    mix_zs, mix_zr, mix_ss, mix,
    turn, hpad, ahead, behind, xpad, pairs, sums, folded, ypad, piece, xs_buf, toep, gated_t,
    sib_out, sib_in, own, right_out, right_in, right_far, left_out, left_in, left_far,
    load_sem, halo_sem, bias_sem,
    xy_send, xy_recv, z_send, z_recv, kv_send, kv_recv, back_send, back_recv,
    sib_send, sib_recv, right_send, right_recv, left_send, left_recv,
):
    context = lax.axis_index("context")
    tensor = lax.axis_index("tensor")
    x = lax.div(context, 16)
    y = lax.rem(context, 4)
    z_hi = lax.rem(lax.div(context, 4), 4)
    z_lo = lax.div(tensor, 2)
    core = lax.rem(tensor, 2)
    here = x * 4 + y

    def plane(step):
        to_x = lax.rem(x + step // 4, 4)
        to_y = lax.rem(y + step % 4, 4)
        return to_x * 4 + to_y, (to_x * 16 + z_hi * 4 + to_y, tensor)

    opposite = lax.rem(z_lo + 4, 8) * 2 + core

    def across(target_hi):
        return (x * 16 + target_hi * 4 + y, opposite)

    def along(target_lo):
        return (context, target_lo * 2 + core)

    after = (lax.rem(context + 1, 64), tensor)
    before = (lax.rem(context + 63, 64), tensor)
    sibling = (context, z_lo * 2 + 1 - core)
    right = along(lax.rem(z_lo + 1, 8))
    left = along(lax.rem(z_lo + 7, 8))

    def swap_blocks(src, dst):
        for half in range(2):
            lanes = pl.ds(half * LANES, LANES)
            turn[half] = src[:, lanes].astype(F32)
        for j in range(16):
            for half in range(2):
                block = turn[half, pl.ds(j, 16, stride=16), :]
                dst[pl.ds(16 * j, 16), pl.ds(half * LANES, LANES)] = block.astype(BF16)

    loads = [
        pltpu.make_async_copy(feat_hbm, feat, load_sem.at[0]),
        pltpu.make_async_copy(filt_hbm, filt, load_sem.at[1]),
        pltpu.make_async_copy(w_hbm, w, load_sem.at[2]),
        pltpu.make_async_copy(taps_hbm, taps, load_sem.at[3]),
        pltpu.make_async_copy(bias_hbm, bias_out, load_sem.at[4]),
    ]
    for which in (1, 0, 3, 4, 2):
        loads[which].start()

    barrier = pltpu.get_barrier_semaphore()
    peers = [across(lax.rem(z_hi + step, 4)) for step in (2, 1, 3, 0)]
    peers += [before]
    peers += [along(lax.rem(z_lo + step, 8)) for step in range(1, 8)]
    peers += [plane(step)[1] for step in range(1, 16)]
    peers += [sibling]
    for peer in peers:
        pl.semaphore_signal(barrier, inc=1, device_id=peer, device_id_type=MESH)

    loads[1].wait()
    swap_blocks(filt, filt_pre)
    for which in (0, 3, 4):
        loads[which].wait()

    row = lax.broadcasted_iota(jnp.int32, (16, SIDE), 0)
    pos = lax.broadcasted_iota(jnp.int32, (16, SIDE), 1)
    edge = jnp.zeros((16, SIDE), F32)
    for stream in range(3):
        pick = ((row - 2 * stream == pos - (SIDE - 2)) & (pos >= SIDE - 2)).astype(F32).astype(BF16)
        edge = edge + lax.dot_general(
            pick, feat[stream], (((1,), (1,)), ((), ())), preferred_element_type=F32
        )
    halo_out[...] = edge.astype(BF16)
    cols[...] = jnp.zeros((LANES, SIDE), F32)
    for stream in range(3):
        for tap in range(3):
            cols[pl.ds(3 * stream + tap, 1), :] = taps[stream, pl.ds(tap, 1), :]
    hpad[:, 0:8, :] = jnp.zeros((4, 8, LANES), F32)
    xpad[:, 0:8, :] = jnp.zeros((4, 8, LANES), F32)
    pairs[0:32, :] = jnp.zeros((32, LANES), F32)
    sums[0:32, :] = jnp.zeros((32, LANES), F32)

    pl.semaphore_wait(barrier, len(peers))

    sent = []
    halo_copy = remote(halo_out, halo_in, halo_sem.at[0], halo_sem.at[1], after)
    halo_copy.start()
    bias_copy = remote(bias_out, bias_in, bias_sem.at[0], bias_sem.at[1], across(z_hi))
    bias_copy.start()

    sent.extend([halo_copy, bias_copy])

    def plane_exchange(src, dst, which):
        copies = []
        for step in range(1, 16):
            to, device = plane(step)
            copy = remote(
                src.at[pl.ds(pl.multiple_of(to * 16, 16), 16)],
                dst.at[pl.ds(pl.multiple_of(here * 16, 16), 16)],
                xy_send.at[which, step], xy_recv.at[which, step], device,
            )
            copy.start()
            copies.append(copy)
        mine = pl.ds(pl.multiple_of(here * 16, 16), 16)
        dst[mine, :] = src[mine, :]
        sent.extend(copies)
        return copies

    def across_exchange(src, dst, send, recv, first, rows):
        copies = []
        for step in (2, 1, 3, 0):
            to = lax.rem(z_hi + step, 4)
            copy = remote(
                src.at[pl.ds(pl.multiple_of(to * 64 + first, 16), rows)],
                dst.at[pl.ds(pl.multiple_of(z_hi * 64 + first, 16), rows)],
                send.at[step], recv.at[step], across(to),
            )
            copy.start()
            copies.append(copy)
        sent.extend(copies)
        return copies

    def arrived(copies):
        for copy in copies:
            copy.wait_recv()

    def spread(src, dst, start, ch):
        for zs in range(4):
            tile = src[pl.ds(zs * 64 + ch * 16, 16), :].astype(F32)
            for xs in range(4):
                for half in range(2):
                    first = start + (xs * 16 + zs * 4) * 2 + half
                    dst[ch, pl.ds(first, 4, stride=2), :] = tile[
                        4 * xs : 4 * xs + 4, half * LANES : (half + 1) * LANES
                    ]

    filt_across = across_exchange(filt_pre, filt_zr, z_send, z_recv, 0, 64)

    halo_copy.wait_recv()
    seen = jnp.where(context > 0, 1.0, 0.0)
    cols[16:32, :] = halo_in[...].astype(F32) * seen
    turned = cols[...].T
    lane = lax.broadcasted_iota(jnp.int32, (64, SIDE), 1)
    for block in range(4):
        rows = slice(64 * block, 64 * block + 64)
        shaped = []
        for stream in range(3):
            now = feat[stream, rows, :].astype(F32)
            last = turned[rows, 16 + 2 * stream + 1 : 16 + 2 * stream + 2]
            older = turned[rows, 16 + 2 * stream : 16 + 2 * stream + 1]
            one = jnp.where(lane == 0, last, pltpu.roll(now, 1, 1))
            two = jnp.where(lane == 0, older, jnp.where(lane == 1, last, pltpu.roll(now, 2, 1)))
            tap = [turned[rows, 3 * stream + j : 3 * stream + j + 1] for j in range(3)]
            shaped.append(tap[0] * now + tap[1] * one + tap[2] * two)
        gate[rows, :] = shaped[0].astype(BF16)
        kv[rows, :] = (shaped[1] * shaped[2]).astype(BF16)

    kv_plane = plane_exchange(kv, kv_xy, 1)
    arrived(kv_plane)
    swap_blocks(kv_xy, kv_zs)
    kv_across = [
        across_exchange(kv_zs, kv_zr, kv_send.at[ch], kv_recv.at[ch], 16 * ch, 16)
        for ch in range(4)
    ]

    arrived(filt_across)
    swap_blocks(filt_zr, filt_zs)
    arrived(plane_exchange(filt_zs, filt_xy, 0))
    swap_blocks(filt_xy, filt_all)
    for ch in range(4):
        spread(filt_all, hpad, 8, ch)

    low = lax.broadcasted_iota(jnp.int32, (16, LANES), 1) < 64
    for ch in range(4):
        for a in range(4):
            one = hpad[ch, pl.ds(8 + 32 * a, 16), :]
            two = hpad[ch, pl.ds(24 + 32 * a, 16), :]
            even = jnp.where(low, one, pltpu.roll(two, 64, 1))
            odd = jnp.where(low, pltpu.roll(one, 64, 1), two)
            ahead[ch, pl.ds(32 * a, 16, stride=2), :] = even
            ahead[ch, pl.ds(32 * a + 1, 16, stride=2), :] = odd
            behind[ch, pl.ds(32 * a + 1, 16, stride=2), :] = pltpu.roll(even, 64, 1)
            behind[ch, pl.ds(32 * a + 2, 16, stride=2), :] = pltpu.roll(odd, 64, 1)
        for a in range(4):
            one = hpad[ch, pl.ds(23 + 32 * a, 1), :]
            two = hpad[ch, pl.ds(7 + 32 * a, 1), :]
            behind[ch, pl.ds(32 * a, 1), :] = jnp.where(low[:1], pltpu.roll(one, 64, 1), two)
    lane = lax.broadcasted_iota(jnp.int32, (64, LANES), 1)
    down = lax.broadcasted_iota(jnp.int32, (64, LANES), 0)
    keep = lax.rem(lane, 64) + down < 64

    def build(index, carry):
        ch = lax.div(index, 32)
        b = lax.rem(index, 32)
        for a in range(4):
            block = jnp.where(
                keep,
                jnp.broadcast_to(ahead[ch, pl.ds(32 * a + b, 1), :], (64, LANES)),
                jnp.broadcast_to(behind[ch, pl.ds(32 * a + b, 1), :], (64, LANES)),
            )
            block = pltpu.roll(block, 0, 1, stride=1, stride_axis=0)
            toep[ch, pl.ds(pl.multiple_of(b * 64, 64), 64), pl.ds(a * LANES, LANES)] = (
                block.astype(BF16)
            )
        return carry

    lax.fori_loop(0, 128, build, 0)

    bias_copy.wait_recv()
    spot = lax.broadcasted_iota(jnp.int32, (1, SIDE), 1)
    first_lanes = lax.broadcasted_iota(jnp.int32, (LANES, LANES), 1) < 64
    back = ([], [])

    def send_back(half, ch):
        back[half].extend(across_exchange(
            mix_zs.at[half], mix_zr.at[half], back_send.at[half, ch], back_recv.at[half, ch],
            16 * ch, 16,
        ))

    for ch in range(4):
        arrived(kv_across[ch])
        spread(kv_zr, xpad, 8, ch)
        own_row = xpad[ch, pl.ds(8, LANES), :]
        row_before = xpad[ch, pl.ds(7, LANES), :]
        pairs[pl.ds(32, LANES, stride=2), :] = jnp.where(first_lanes, own_row, row_before)
        pairs[pl.ds(33, LANES, stride=2), :] = pltpu.roll(own_row, 64, 1)
        for b in range(16):
            xs_buf[:, pl.ds(b * LANES, LANES)] = pairs[pl.ds(32 - 2 * b, SIDE), :].astype(BF16)
        upper = jnp.dot(xs_buf[...], toep[ch, :, pl.ds(0, SIDE)], preferred_element_type=F32)
        lower = jnp.dot(
            xs_buf[pl.ds(0, LANES), :], toep[ch, :, pl.ds(SIDE, SIDE)],
            preferred_element_type=F32,
        )
        sums[pl.ds(32, SIDE), :] = upper[:, :LANES]
        sums[pl.ds(96, 192), :] += upper[:192, LANES:]
        sums[pl.ds(160, LANES), :] += lower[:, :LANES]
        sums[pl.ds(224, 64), :] += lower[:64, LANES:]
        folded[...] = sums[pl.ds(32, SIDE), :] + pltpu.roll(sums[pl.ds(0, SIDE), :], 64, 1)
        total = jnp.where(
            first_lanes,
            folded[pl.ds(0, LANES, stride=2), :],
            pltpu.roll(folded[pl.ds(1, LANES, stride=2), :], 64, 1),
        )
        channel = here * 16 + z_hi * 4 + ch
        bias = jnp.sum(jnp.where(spot == channel, bias_in[...], 0.0), axis=1, keepdims=True)
        ypad[...] = total + bias * own_row
        for zs in range(4):
            for half in range(2):
                for xs in range(4):
                    piece[pl.ds(4 * xs, 4), :] = ypad[
                        pl.ds((xs * 16 + zs * 4) * 2 + half, 4, stride=2), :
                    ]
                mix_zs[half, pl.ds(zs * 64 + ch * 16, 16), :] = piece[...].astype(BF16)
        send_back(0, ch)
        if ch < 2:
            send_back(1, ch)
    send_back(1, 2)
    send_back(1, 3)

    def sib_copy(half, d):
        rows = pl.ds(half * LANES, LANES)
        return remote(
            sib_out.at[d, rows], sib_in.at[d, rows],
            sib_send.at[half, d], sib_recv.at[half, d], sibling,
        )

    def swap_half(half):
        turn[half] = mix_zr[half].astype(F32)
        for j in range(16):
            mix_ss[half, pl.ds(16 * j, 16), :] = turn[half, pl.ds(j, 16, stride=16), :].astype(BF16)

    def to_plane(half):
        arrived(back[half])
        swap_half(half)
        return plane_exchange(mix_ss.at[half], mix.at[half], 2 + half)

    def project(half):
        lanes = pl.ds(half * LANES, LANES)
        rows = pl.ds(half * LANES, LANES)
        gated = gate[:, lanes].astype(F32) * mix[half].astype(F32)
        gated_t[rows, :] = gated.astype(BF16).astype(F32).T.astype(BF16)
        for d in (7, 0, 6, 1, 5, 2, 4, 3):
            theirs = pl.ds(pl.multiple_of((2 * d + 1 - core) * SIDE, SIDE), SIDE)
            mine = pl.ds(pl.multiple_of((2 * d + core) * SIDE, SIDE), SIDE)
            sib_out[d, rows, :] = jnp.dot(
                gated_t[rows, :], w[:, theirs], preferred_element_type=F32
            ).astype(BF16)
            sib_copy(half, d).start()
            own[d, rows, :] = jnp.dot(gated_t[rows, :], w[:, mine], preferred_element_type=F32)

    size = LANES // PARTS

    def rows_of(half, n):
        return pl.ds(pl.multiple_of(half * LANES + lax.rem(n, PARTS) * size, size), size)

    quarter = lax.rem(z_lo, 4)

    def right_copy(half, n):
        d = 7 - lax.div(n, PARTS)
        return remote(
            right_out.at[d, rows_of(half, n)], right_in.at[d, rows_of(half, n)],
            right_send.at[half, n], right_recv.at[half, n], right,
        )

    def right_jump(half, n, d):
        return remote(
            right_out.at[7 - lax.div(n, PARTS), rows_of(half, n)], right_far.at[rows_of(half, n)],
            right_send.at[half, n], right_recv.at[half, STEPS + lax.rem(n, PARTS)], along(d),
        )

    def left_copy(half, n):
        d = lax.div(n, PARTS)
        return remote(
            left_out.at[d, rows_of(half, n)], left_in.at[d, rows_of(half, n)],
            left_send.at[half, n], left_recv.at[half, n], left,
        )

    def left_jump(half, n, d):
        return remote(
            left_out.at[lax.div(n, PARTS), rows_of(half, n)], left_far.at[rows_of(half, n)],
            left_send.at[half, n], left_recv.at[half, STEPS + lax.rem(n, PARTS)], along(d),
        )

    def pass_on(half, n, d, first, jumps, copy, jump, came, going):
        rows = rows_of(half, n)

        @pl.when(lax.rem(n, PARTS) == 0)
        def _():
            sib_copy(half, d).wait_recv()

        @pl.when(first)
        def _():
            going[d, rows, :] = (own[d, rows, :] + sib_in[d, rows, :].astype(F32)).astype(BF16)

        @pl.when(jnp.logical_not(first))
        def _():
            copy.wait_recv()
            going[d, rows, :] = (
                own[d, rows, :] + sib_in[d, rows, :].astype(F32) + came[d, rows, :].astype(F32)
            ).astype(BF16)

        @pl.when(jumps)
        def _():
            jump.start()

        @pl.when(jnp.logical_not(jumps))
        def _():
            copy.start()

    def reduce_half(half):
        def reduce_step(moment, carry):
            n = moment - quarter * LAG

            @pl.when((n >= 0) & (n < (7 - z_lo) * PARTS))
            def _():
                d = 7 - lax.div(n, PARTS)
                pass_on(
                    half, n, d, quarter == 0, (z_lo == 3) & (d > 4),
                    right_copy(half, n), right_jump(half, n, d), right_in, right_out,
                )

            m = moment - (3 - quarter) * LAG

            @pl.when((m >= 0) & (m < z_lo * PARTS))
            def _():
                d = lax.div(m, PARTS)
                pass_on(
                    half, m, d, quarter == 3, (z_lo == 4) & (d < 3),
                    left_copy(half, m), left_jump(half, m, d), left_in, left_out,
                )

            return carry

        lax.fori_loop(0, STEPS + 3 * LAG, reduce_step, 0)

    first_plane = to_plane(0)
    arrived(first_plane)
    loads[2].wait()
    project(0)
    second_plane = to_plane(1)
    reduce_half(0)
    arrived(second_plane)
    project(1)
    reduce_half(1)

    for half in range(2):
        rows = pl.ds(half * LANES, LANES)
        sib_copy(half, z_lo).wait_recv()
        own[z_lo, rows, :] += sib_in[z_lo, rows, :].astype(F32)

        @pl.when(z_lo > 0)
        def _():
            for part in range(PARTS):
                right_copy(half, (7 - z_lo) * PARTS + part).wait_recv()
            own[z_lo, rows, :] += right_in[z_lo, rows, :].astype(F32)

        @pl.when(z_lo < 7)
        def _():
            for part in range(PARTS):
                left_copy(half, z_lo * PARTS + part).wait_recv()
            own[z_lo, rows, :] += left_in[z_lo, rows, :].astype(F32)

        @pl.when(z_lo > 4)
        def _():
            for part in range(PARTS):
                right_jump(half, part, z_lo).wait_recv()
            own[z_lo, rows, :] += right_far[rows, :].astype(F32)

        @pl.when(z_lo < 3)
        def _():
            for part in range(PARTS):
                left_jump(half, part, z_lo).wait_recv()
            own[z_lo, rows, :] += left_far[rows, :].astype(F32)

    out_ref[...] = own[z_lo].astype(BF16)

    for copy in sent:
        copy.wait_send()
    for half in range(2):
        for d in range(8):
            sib_copy(half, d).wait_send()

        def close(n, carry):
            @pl.when(n < (7 - z_lo) * PARTS)
            def _():
                right_copy(half, n).wait_send()

            @pl.when(n < z_lo * PARTS)
            def _():
                left_copy(half, n).wait_send()

            return carry

        lax.fori_loop(0, STEPS, close, 0)


def local(features, short_taps, long_filter, skip_bias, out_weight):
    vmem = pl.BlockSpec(memory_space=pltpu.VMEM)
    anywhere = pl.BlockSpec(memory_space=pl.ANY)
    square = pltpu.VMEM((SIDE, SIDE), BF16)
    halves = pltpu.VMEM((2, SIDE, LANES), BF16)
    dma = pltpu.SemaphoreType.DMA
    return pl.pallas_call(
        kernel,
        out_shape=jax.ShapeDtypeStruct((SIDE, SIDE), BF16),
        in_specs=[anywhere] * 5,
        out_specs=vmem,
        scratch_shapes=[
            pltpu.VMEM((3, SIDE, SIDE), BF16),
            pltpu.VMEM((3, 3, SIDE), F32),
            square,
            pltpu.VMEM((1, SIDE), F32),
            pltpu.VMEM((SIDE, 16 * SIDE), BF16),
            pltpu.VMEM((LANES, SIDE), F32),
            pltpu.VMEM((16, SIDE), BF16),
            pltpu.VMEM((16, SIDE), BF16),
            pltpu.VMEM((1, SIDE), F32),
            square, square,
            square, square, square, square, square,
            square, square, square,
            halves, halves, halves, halves,
            pltpu.VMEM((2, SIDE, LANES), F32),
            pltpu.VMEM((4, 136, LANES), F32),
            pltpu.VMEM((4, LANES, LANES), F32),
            pltpu.VMEM((4, 136, LANES), F32),
            pltpu.VMEM((4, 136, LANES), F32),
            pltpu.VMEM((32 + SIDE, LANES), F32),
            pltpu.VMEM((32 + SIDE, LANES), F32),
            pltpu.VMEM((SIDE, LANES), F32),
            pltpu.VMEM((LANES, LANES), F32),
            pltpu.VMEM((16, LANES), F32),
            pltpu.VMEM((SIDE, 2048), BF16),
            pltpu.VMEM((4, 2048, 512), BF16),
            square,
            pltpu.VMEM((8, SIDE, SIDE), BF16),
            pltpu.VMEM((8, SIDE, SIDE), BF16),
            pltpu.VMEM((8, SIDE, SIDE), F32),
            pltpu.VMEM((8, SIDE, SIDE), BF16), pltpu.VMEM((8, SIDE, SIDE), BF16), square,
            pltpu.VMEM((8, SIDE, SIDE), BF16), pltpu.VMEM((8, SIDE, SIDE), BF16), square,
            dma((5,)), dma((2,)), dma((2,)),
            dma((4, 16)), dma((4, 16)),
            dma((4,)), dma((4,)),
            dma((4, 4)), dma((4, 4)),
            dma((2, 4, 4)), dma((2, 4, 4)),
            dma((2, 8)), dma((2, 8)),
            dma((2, STEPS)), dma((2, STEPS + PARTS)),
            dma((2, STEPS)), dma((2, STEPS + PARTS)),
        ],
        compiler_params=pltpu.CompilerParams(
            collective_id=0, has_side_effects=True, vmem_limit_bytes=60 << 20
        ),
        cost_estimate=pl.CostEstimate(
            flops=4 * 10**9, bytes_accessed=3 * 10**6, transcendentals=0
        ),
        name="hyena_operator",
    )(features, short_taps, long_filter, skip_bias.reshape(1, SIDE), out_weight)


def solution(mesh):
    placed = (
        P(None, "tensor", "context"),
        P(None, None, "tensor"),
        P("tensor", "context"),
        P("tensor"),
        P("tensor", None),
    )
    return jax.shard_map(
        local, mesh=mesh, in_specs=placed, out_specs=P("context", "tensor"), check_vma=False
    )
```

```python
import jax
import jax.numpy as jnp
from jax import lax
from jax.experimental import pallas as pl
from jax.experimental.pallas import tpu as pltpu
from jax.sharding import PartitionSpec as P

MESH = pl.DeviceIdType.MESH
F32 = jnp.float32
BF16 = jnp.bfloat16
SIDE = 256
LANES = 128
PARTS = 2
LAG = 4
STEPS = 7 * PARTS


def remote(src, dst, send_sem, recv_sem, device):
    return pltpu.make_async_remote_copy(
        src_ref=src, dst_ref=dst, send_sem=send_sem, recv_sem=recv_sem,
        device_id=device, device_id_type=MESH,
    )


def kernel(
    feat_hbm, taps_hbm, filt_hbm, bias_hbm, w_hbm, out_ref,
    feat, taps, filt, bias_out, w, cols, halo_out, halo_in, bias_in, gate, kv,
    filt_pre, filt_zr, filt_zs, filt_xy, filt_all, kv_xy, kv_zs, kv_zr,
    mix_zs, mix_zr, mix_ss, mix,
    turn, hpad, ahead, behind, xpad, pairs, sums, folded, ypad, piece, xs_buf, toep, gated_t,
    sib_out, sib_in, own, right_out, right_in, right_far, left_out, left_in, left_far,
    load_sem, halo_sem, bias_sem,
    xy_send, xy_recv, z_send, z_recv, kv_send, kv_recv, back_send, back_recv,
    sib_send, sib_recv, right_send, right_recv, left_send, left_recv,
):
    context = lax.axis_index("context")
    tensor = lax.axis_index("tensor")
    x = lax.div(context, 16)
    y = lax.rem(context, 4)
    z_hi = lax.rem(lax.div(context, 4), 4)
    z_lo = lax.div(tensor, 2)
    core = lax.rem(tensor, 2)
    here = x * 4 + y

    def plane(step):
        to_x = lax.rem(x + step // 4, 4)
        to_y = lax.rem(y + step % 4, 4)
        return to_x * 4 + to_y, (to_x * 16 + z_hi * 4 + to_y, tensor)

    opposite = lax.rem(z_lo + 4, 8) * 2 + core

    def across(target_hi):
        return (x * 16 + target_hi * 4 + y, opposite)

    def along(target_lo):
        return (context, target_lo * 2 + core)

    after = (lax.rem(context + 1, 64), tensor)
    before = (lax.rem(context + 63, 64), tensor)
    sibling = (context, z_lo * 2 + 1 - core)
    right = along(lax.rem(z_lo + 1, 8))
    left = along(lax.rem(z_lo + 7, 8))

    def swap_blocks(src, dst):
        for half in range(2):
            lanes = pl.ds(half * LANES, LANES)
            turn[half] = src[:, lanes].astype(F32)
        for j in range(16):
            for half in range(2):
                block = turn[half, pl.ds(j, 16, stride=16), :]
                dst[pl.ds(16 * j, 16), pl.ds(half * LANES, LANES)] = block.astype(BF16)

    loads = [
        pltpu.make_async_copy(feat_hbm, feat, load_sem.at[0]),
        pltpu.make_async_copy(filt_hbm, filt, load_sem.at[1]),
        pltpu.make_async_copy(w_hbm, w, load_sem.at[2]),
        pltpu.make_async_copy(taps_hbm, taps, load_sem.at[3]),
        pltpu.make_async_copy(bias_hbm, bias_out, load_sem.at[4]),
    ]
    for which in (1, 0, 3, 4, 2):
        loads[which].start()

    barrier = pltpu.get_barrier_semaphore()
    peers = [across(lax.rem(z_hi + step, 4)) for step in (2, 1, 3, 0)]
    peers += [before]
    peers += [along(lax.rem(z_lo + step, 8)) for step in range(1, 8)]
    peers += [plane(step)[1] for step in range(1, 16)]
    peers += [sibling]
    for peer in peers:
        pl.semaphore_signal(barrier, inc=1, device_id=peer, device_id_type=MESH)

    loads[1].wait()
    swap_blocks(filt, filt_pre)
    for which in (0, 3, 4):
        loads[which].wait()

    row = lax.broadcasted_iota(jnp.int32, (16, SIDE), 0)
    pos = lax.broadcasted_iota(jnp.int32, (16, SIDE), 1)
    edge = jnp.zeros((16, SIDE), F32)
    for stream in range(3):
        pick = ((row - 2 * stream == pos - (SIDE - 2)) & (pos >= SIDE - 2)).astype(F32).astype(BF16)
        edge = edge + lax.dot_general(
            pick, feat[stream], (((1,), (1,)), ((), ())), preferred_element_type=F32
        )
    halo_out[...] = edge.astype(BF16)
    cols[...] = jnp.zeros((LANES, SIDE), F32)
    for stream in range(3):
        for tap in range(3):
            cols[pl.ds(3 * stream + tap, 1), :] = taps[stream, pl.ds(tap, 1), :]
    hpad[:, 0:8, :] = jnp.zeros((4, 8, LANES), F32)
    xpad[:, 0:8, :] = jnp.zeros((4, 8, LANES), F32)
    pairs[0:32, :] = jnp.zeros((32, LANES), F32)
    sums[0:32, :] = jnp.zeros((32, LANES), F32)

    pl.semaphore_wait(barrier, len(peers))

    sent = []
    halo_copy = remote(halo_out, halo_in, halo_sem.at[0], halo_sem.at[1], after)
    halo_copy.start()
    bias_copy = remote(bias_out, bias_in, bias_sem.at[0], bias_sem.at[1], across(z_hi))
    bias_copy.start()

    sent.extend([halo_copy, bias_copy])

    def plane_exchange(src, dst, which):
        copies = []
        for step in range(1, 16):
            to, device = plane(step)
            copy = remote(
                src.at[pl.ds(pl.multiple_of(to * 16, 16), 16)],
                dst.at[pl.ds(pl.multiple_of(here * 16, 16), 16)],
                xy_send.at[which, step], xy_recv.at[which, step], device,
            )
            copy.start()
            copies.append(copy)
        mine = pl.ds(pl.multiple_of(here * 16, 16), 16)
        dst[mine, :] = src[mine, :]
        sent.extend(copies)
        return copies

    def across_exchange(src, dst, send, recv, first, rows):
        copies = []
        for step in (2, 1, 3, 0):
            to = lax.rem(z_hi + step, 4)
            copy = remote(
                src.at[pl.ds(pl.multiple_of(to * 64 + first, 16), rows)],
                dst.at[pl.ds(pl.multiple_of(z_hi * 64 + first, 16), rows)],
                send.at[step], recv.at[step], across(to),
            )
            copy.start()
            copies.append(copy)
        sent.extend(copies)
        return copies

    def arrived(copies):
        for copy in copies:
            copy.wait_recv()

    def spread(src, dst, start, ch):
        for zs in range(4):
            tile = src[pl.ds(zs * 64 + ch * 16, 16), :].astype(F32)
            for xs in range(4):
                for half in range(2):
                    first = start + (xs * 16 + zs * 4) * 2 + half
                    dst[ch, pl.ds(first, 4, stride=2), :] = tile[
                        4 * xs : 4 * xs + 4, half * LANES : (half + 1) * LANES
                    ]

    filt_across = across_exchange(filt_pre, filt_zr, z_send, z_recv, 0, 64)

    halo_copy.wait_recv()
    seen = jnp.where(context > 0, 1.0, 0.0)
    cols[16:32, :] = halo_in[...].astype(F32) * seen
    turned = cols[...].T
    lane = lax.broadcasted_iota(jnp.int32, (64, SIDE), 1)
    for block in range(4):
        rows = slice(64 * block, 64 * block + 64)
        shaped = []
        for stream in range(3):
            now = feat[stream, rows, :].astype(F32)
            last = turned[rows, 16 + 2 * stream + 1 : 16 + 2 * stream + 2]
            older = turned[rows, 16 + 2 * stream : 16 + 2 * stream + 1]
            one = jnp.where(lane == 0, last, pltpu.roll(now, 1, 1))
            two = jnp.where(lane == 0, older, jnp.where(lane == 1, last, pltpu.roll(now, 2, 1)))
            tap = [turned[rows, 3 * stream + j : 3 * stream + j + 1] for j in range(3)]
            shaped.append(tap[0] * now + tap[1] * one + tap[2] * two)
        gate[rows, :] = shaped[0].astype(BF16)
        kv[rows, :] = (shaped[1] * shaped[2]).astype(BF16)

    kv_plane = plane_exchange(kv, kv_xy, 1)
    arrived(kv_plane)
    swap_blocks(kv_xy, kv_zs)
    kv_across = [
        across_exchange(kv_zs, kv_zr, kv_send.at[ch], kv_recv.at[ch], 16 * ch, 16)
        for ch in range(4)
    ]

    arrived(filt_across)
    swap_blocks(filt_zr, filt_zs)
    arrived(plane_exchange(filt_zs, filt_xy, 0))
    swap_blocks(filt_xy, filt_all)
    for ch in range(4):
        spread(filt_all, hpad, 8, ch)

    low = lax.broadcasted_iota(jnp.int32, (16, LANES), 1) < 64
    for ch in range(4):
        for a in range(4):
            one = hpad[ch, pl.ds(8 + 32 * a, 16), :]
            two = hpad[ch, pl.ds(24 + 32 * a, 16), :]
            even = jnp.where(low, one, pltpu.roll(two, 64, 1))
            odd = jnp.where(low, pltpu.roll(one, 64, 1), two)
            ahead[ch, pl.ds(32 * a, 16, stride=2), :] = even
            ahead[ch, pl.ds(32 * a + 1, 16, stride=2), :] = odd
            behind[ch, pl.ds(32 * a + 1, 16, stride=2), :] = pltpu.roll(even, 64, 1)
            behind[ch, pl.ds(32 * a + 2, 16, stride=2), :] = pltpu.roll(odd, 64, 1)
        for a in range(4):
            one = hpad[ch, pl.ds(23 + 32 * a, 1), :]
            two = hpad[ch, pl.ds(7 + 32 * a, 1), :]
            behind[ch, pl.ds(32 * a, 1), :] = jnp.where(low[:1], pltpu.roll(one, 64, 1), two)
    lane = lax.broadcasted_iota(jnp.int32, (64, LANES), 1)
    down = lax.broadcasted_iota(jnp.int32, (64, LANES), 0)
    keep = lax.rem(lane, 64) + down < 64

    def build(index, carry):
        ch = lax.div(index, 32)
        b = lax.rem(index, 32)
        for a in range(4):
            block = jnp.where(
                keep,
                jnp.broadcast_to(ahead[ch, pl.ds(32 * a + b, 1), :], (64, LANES)),
                jnp.broadcast_to(behind[ch, pl.ds(32 * a + b, 1), :], (64, LANES)),
            )
            block = pltpu.roll(block, 0, 1, stride=1, stride_axis=0)
            toep[ch, pl.ds(pl.multiple_of(b * 64, 64), 64), pl.ds(a * LANES, LANES)] = (
                block.astype(BF16)
            )
        return carry

    lax.fori_loop(0, 128, build, 0)

    bias_copy.wait_recv()
    spot = lax.broadcasted_iota(jnp.int32, (1, SIDE), 1)
    first_lanes = lax.broadcasted_iota(jnp.int32, (LANES, LANES), 1) < 64
    back = ([], [])

    def send_back(half, ch):
        back[half].extend(across_exchange(
            mix_zs.at[half], mix_zr.at[half], back_send.at[half, ch], back_recv.at[half, ch],
            16 * ch, 16,
        ))

    for ch in range(4):
        arrived(kv_across[ch])
        spread(kv_zr, xpad, 8, ch)
        own_row = xpad[ch, pl.ds(8, LANES), :]
        row_before = xpad[ch, pl.ds(7, LANES), :]
        pairs[pl.ds(32, LANES, stride=2), :] = jnp.where(first_lanes, own_row, row_before)
        pairs[pl.ds(33, LANES, stride=2), :] = pltpu.roll(own_row, 64, 1)
        for b in range(16):
            xs_buf[:, pl.ds(b * LANES, LANES)] = pairs[pl.ds(32 - 2 * b, SIDE), :].astype(BF16)
        upper = jnp.dot(xs_buf[...], toep[ch, :, pl.ds(0, SIDE)], preferred_element_type=F32)
        lower = jnp.dot(
            xs_buf[pl.ds(0, LANES), :], toep[ch, :, pl.ds(SIDE, SIDE)],
            preferred_element_type=F32,
        )
        sums[pl.ds(32, SIDE), :] = upper[:, :LANES]
        sums[pl.ds(96, 192), :] += upper[:192, LANES:]
        sums[pl.ds(160, LANES), :] += lower[:, :LANES]
        sums[pl.ds(224, 64), :] += lower[:64, LANES:]
        folded[...] = sums[pl.ds(32, SIDE), :] + pltpu.roll(sums[pl.ds(0, SIDE), :], 64, 1)
        total = jnp.where(
            first_lanes,
            folded[pl.ds(0, LANES, stride=2), :],
            pltpu.roll(folded[pl.ds(1, LANES, stride=2), :], 64, 1),
        )
        channel = here * 16 + z_hi * 4 + ch
        bias = jnp.sum(jnp.where(spot == channel, bias_in[...], 0.0), axis=1, keepdims=True)
        ypad[...] = total + bias * own_row
        for zs in range(4):
            for half in range(2):
                for xs in range(4):
                    piece[pl.ds(4 * xs, 4), :] = ypad[
                        pl.ds((xs * 16 + zs * 4) * 2 + half, 4, stride=2), :
                    ]
                mix_zs[half, pl.ds(zs * 64 + ch * 16, 16), :] = piece[...].astype(BF16)
        send_back(0, ch)
        if ch < 2:
            send_back(1, ch)
    send_back(1, 2)
    send_back(1, 3)

    def sib_copy(half, d):
        rows = pl.ds(half * LANES, LANES)
        return remote(
            sib_out.at[d, rows], sib_in.at[d, rows],
            sib_send.at[half, d], sib_recv.at[half, d], sibling,
        )

    def swap_half(half):
        turn[half] = mix_zr[half].astype(F32)
        for j in range(16):
            mix_ss[half, pl.ds(16 * j, 16), :] = turn[half, pl.ds(j, 16, stride=16), :].astype(BF16)

    def to_plane(half):
        arrived(back[half])
        swap_half(half)
        return plane_exchange(mix_ss.at[half], mix.at[half], 2 + half)

    def project(half):
        lanes = pl.ds(half * LANES, LANES)
        rows = pl.ds(half * LANES, LANES)
        gated = gate[:, lanes].astype(F32) * mix[half].astype(F32)
        gated_t[rows, :] = gated.astype(BF16).astype(F32).T.astype(BF16)
        for d in (7, 0, 6, 1, 5, 2, 4, 3):
            theirs = pl.ds(pl.multiple_of((2 * d + 1 - core) * SIDE, SIDE), SIDE)
            mine = pl.ds(pl.multiple_of((2 * d + core) * SIDE, SIDE), SIDE)
            sib_out[d, rows, :] = jnp.dot(
                gated_t[rows, :], w[:, theirs], preferred_element_type=F32
            ).astype(BF16)
            sib_copy(half, d).start()
            own[d, rows, :] = jnp.dot(gated_t[rows, :], w[:, mine], preferred_element_type=F32)

    size = LANES // PARTS

    def rows_of(half, n):
        return pl.ds(pl.multiple_of(half * LANES + lax.rem(n, PARTS) * size, size), size)

    quarter = lax.rem(z_lo, 4)

    def right_copy(half, n):
        d = 7 - lax.div(n, PARTS)
        return remote(
            right_out.at[d, rows_of(half, n)], right_in.at[d, rows_of(half, n)],
            right_send.at[half, n], right_recv.at[half, n], right,
        )

    def right_jump(half, n, d):
        return remote(
            right_out.at[7 - lax.div(n, PARTS), rows_of(half, n)], right_far.at[rows_of(half, n)],
            right_send.at[half, n], right_recv.at[half, STEPS + lax.rem(n, PARTS)], along(d),
        )

    def left_copy(half, n):
        d = lax.div(n, PARTS)
        return remote(
            left_out.at[d, rows_of(half, n)], left_in.at[d, rows_of(half, n)],
            left_send.at[half, n], left_recv.at[half, n], left,
        )

    def left_jump(half, n, d):
        return remote(
            left_out.at[lax.div(n, PARTS), rows_of(half, n)], left_far.at[rows_of(half, n)],
            left_send.at[half, n], left_recv.at[half, STEPS + lax.rem(n, PARTS)], along(d),
        )

    def pass_on(half, n, d, first, jumps, copy, jump, came, going):
        rows = rows_of(half, n)

        @pl.when(lax.rem(n, PARTS) == 0)
        def _():
            sib_copy(half, d).wait_recv()

        @pl.when(first)
        def _():
            going[d, rows, :] = (own[d, rows, :] + sib_in[d, rows, :].astype(F32)).astype(BF16)

        @pl.when(jnp.logical_not(first))
        def _():
            copy.wait_recv()
            going[d, rows, :] = (
                own[d, rows, :] + sib_in[d, rows, :].astype(F32) + came[d, rows, :].astype(F32)
            ).astype(BF16)

        @pl.when(jumps)
        def _():
            jump.start()

        @pl.when(jnp.logical_not(jumps))
        def _():
            copy.start()

    def reduce_step(moment, carry):
        n = moment - quarter * LAG
        n_half = jnp.where(n < STEPS, 0, 1)
        n_here = n - n_half * STEPS

        @pl.when((n >= 0) & (n_here < (7 - z_lo) * PARTS))
        def _():
            d = 7 - lax.div(n_here, PARTS)
            pass_on(
                n_half, n_here, d, quarter == 0, (z_lo == 3) & (d > 4),
                right_copy(n_half, n_here), right_jump(n_half, n_here, d), right_in, right_out,
            )

        m = moment - (3 - quarter) * LAG
        m_half = jnp.where(m < STEPS, 0, 1)
        m_here = m - m_half * STEPS

        @pl.when((m >= 0) & (m_here < z_lo * PARTS))
        def _():
            d = lax.div(m_here, PARTS)
            pass_on(
                m_half, m_here, d, quarter == 3, (z_lo == 4) & (d < 3),
                left_copy(m_half, m_here), left_jump(m_half, m_here, d), left_in, left_out,
            )

        return carry

    first_plane = to_plane(0)
    arrived(first_plane)
    loads[2].wait()
    project(0)
    second_plane = to_plane(1)
    lax.fori_loop(0, STEPS, reduce_step, 0)
    arrived(second_plane)
    project(1)
    lax.fori_loop(STEPS, 2 * STEPS + 3 * LAG, reduce_step, 0)

    for half in range(2):
        rows = pl.ds(half * LANES, LANES)
        sib_copy(half, z_lo).wait_recv()
        own[z_lo, rows, :] += sib_in[z_lo, rows, :].astype(F32)

        @pl.when(z_lo > 0)
        def _():
            for part in range(PARTS):
                right_copy(half, (7 - z_lo) * PARTS + part).wait_recv()
            own[z_lo, rows, :] += right_in[z_lo, rows, :].astype(F32)

        @pl.when(z_lo < 7)
        def _():
            for part in range(PARTS):
                left_copy(half, z_lo * PARTS + part).wait_recv()
            own[z_lo, rows, :] += left_in[z_lo, rows, :].astype(F32)

        @pl.when(z_lo > 4)
        def _():
            for part in range(PARTS):
                right_jump(half, part, z_lo).wait_recv()
            own[z_lo, rows, :] += right_far[rows, :].astype(F32)

        @pl.when(z_lo < 3)
        def _():
            for part in range(PARTS):
                left_jump(half, part, z_lo).wait_recv()
            own[z_lo, rows, :] += left_far[rows, :].astype(F32)

    out_ref[...] = own[z_lo].astype(BF16)

    for copy in sent:
        copy.wait_send()
    for half in range(2):
        for d in range(8):
            sib_copy(half, d).wait_send()

        def close(n, carry):
            @pl.when(n < (7 - z_lo) * PARTS)
            def _():
                right_copy(half, n).wait_send()

            @pl.when(n < z_lo * PARTS)
            def _():
                left_copy(half, n).wait_send()

            return carry

        lax.fori_loop(0, STEPS, close, 0)


def local(features, short_taps, long_filter, skip_bias, out_weight):
    vmem = pl.BlockSpec(memory_space=pltpu.VMEM)
    anywhere = pl.BlockSpec(memory_space=pl.ANY)
    square = pltpu.VMEM((SIDE, SIDE), BF16)
    halves = pltpu.VMEM((2, SIDE, LANES), BF16)
    dma = pltpu.SemaphoreType.DMA
    return pl.pallas_call(
        kernel,
        out_shape=jax.ShapeDtypeStruct((SIDE, SIDE), BF16),
        in_specs=[anywhere] * 5,
        out_specs=vmem,
        scratch_shapes=[
            pltpu.VMEM((3, SIDE, SIDE), BF16),
            pltpu.VMEM((3, 3, SIDE), F32),
            square,
            pltpu.VMEM((1, SIDE), F32),
            pltpu.VMEM((SIDE, 16 * SIDE), BF16),
            pltpu.VMEM((LANES, SIDE), F32),
            pltpu.VMEM((16, SIDE), BF16),
            pltpu.VMEM((16, SIDE), BF16),
            pltpu.VMEM((1, SIDE), F32),
            square, square,
            square, square, square, square, square,
            square, square, square,
            halves, halves, halves, halves,
            pltpu.VMEM((2, SIDE, LANES), F32),
            pltpu.VMEM((4, 136, LANES), F32),
            pltpu.VMEM((4, LANES, LANES), F32),
            pltpu.VMEM((4, 136, LANES), F32),
            pltpu.VMEM((4, 136, LANES), F32),
            pltpu.VMEM((32 + SIDE, LANES), F32),
            pltpu.VMEM((32 + SIDE, LANES), F32),
            pltpu.VMEM((SIDE, LANES), F32),
            pltpu.VMEM((LANES, LANES), F32),
            pltpu.VMEM((16, LANES), F32),
            pltpu.VMEM((SIDE, 2048), BF16),
            pltpu.VMEM((4, 2048, 512), BF16),
            square,
            pltpu.VMEM((8, SIDE, SIDE), BF16),
            pltpu.VMEM((8, SIDE, SIDE), BF16),
            pltpu.VMEM((8, SIDE, SIDE), F32),
            pltpu.VMEM((8, SIDE, SIDE), BF16), pltpu.VMEM((8, SIDE, SIDE), BF16), square,
            pltpu.VMEM((8, SIDE, SIDE), BF16), pltpu.VMEM((8, SIDE, SIDE), BF16), square,
            dma((5,)), dma((2,)), dma((2,)),
            dma((4, 16)), dma((4, 16)),
            dma((4,)), dma((4,)),
            dma((4, 4)), dma((4, 4)),
            dma((2, 4, 4)), dma((2, 4, 4)),
            dma((2, 8)), dma((2, 8)),
            dma((2, STEPS)), dma((2, STEPS + PARTS)),
            dma((2, STEPS)), dma((2, STEPS + PARTS)),
        ],
        compiler_params=pltpu.CompilerParams(
            collective_id=0, has_side_effects=True, vmem_limit_bytes=60 << 20
        ),
        cost_estimate=pl.CostEstimate(
            flops=4 * 10**9, bytes_accessed=3 * 10**6, transcendentals=0
        ),
        name="hyena_operator",
    )(features, short_taps, long_filter, skip_bias.reshape(1, SIDE), out_weight)


def solution(mesh):
    placed = (
        P(None, "tensor", "context"),
        P(None, None, "tensor"),
        P("tensor", "context"),
        P("tensor"),
        P("tensor", None),
    )
    return jax.shard_map(
        local, mesh=mesh, in_specs=placed, out_specs=P("context", "tensor"), check_vma=False
    )
```

```python
import jax
import jax.numpy as jnp
from jax import lax
from jax.experimental import pallas as pl
from jax.experimental.pallas import tpu as pltpu
from jax.sharding import PartitionSpec as P

MESH = pl.DeviceIdType.MESH
F32 = jnp.float32
BF16 = jnp.bfloat16
SIDE = 256
LANES = 128
PARTS = 4
LAG = 4
STEPS = 7 * PARTS


def remote(src, dst, send_sem, recv_sem, device):
    return pltpu.make_async_remote_copy(
        src_ref=src, dst_ref=dst, send_sem=send_sem, recv_sem=recv_sem,
        device_id=device, device_id_type=MESH,
    )


def kernel(
    feat_hbm, taps_hbm, filt_hbm, bias_hbm, w_hbm, out_ref,
    feat, taps, filt, bias_out, w, cols, halo_out, halo_in, bias_in, gate, kv,
    filt_pre, filt_zr, filt_zs, filt_xy, filt_all, kv_xy, kv_zs, kv_zr,
    mix_zs, mix_zr, mix_ss, mix,
    turn, hpad, ahead, behind, xpad, pairs, sums, folded, ypad, piece, xs_buf, toep, gated_t,
    sib_out, sib_in, own, right_out, right_in, right_far, left_out, left_in, left_far,
    load_sem, halo_sem, bias_sem,
    xy_send, xy_recv, z_send, z_recv, kv_send, kv_recv, back_send, back_recv,
    sib_send, sib_recv, right_send, right_recv, left_send, left_recv,
):
    context = lax.axis_index("context")
    tensor = lax.axis_index("tensor")
    x = lax.div(context, 16)
    y = lax.rem(context, 4)
    z_hi = lax.rem(lax.div(context, 4), 4)
    z_lo = lax.div(tensor, 2)
    core = lax.rem(tensor, 2)
    here = x * 4 + y

    def plane(step):
        to_x = lax.rem(x + step // 4, 4)
        to_y = lax.rem(y + step % 4, 4)
        return to_x * 4 + to_y, (to_x * 16 + z_hi * 4 + to_y, tensor)

    opposite = lax.rem(z_lo + 4, 8) * 2 + core

    def across(target_hi):
        return (x * 16 + target_hi * 4 + y, opposite)

    def along(target_lo):
        return (context, target_lo * 2 + core)

    after = (lax.rem(context + 1, 64), tensor)
    before = (lax.rem(context + 63, 64), tensor)
    sibling = (context, z_lo * 2 + 1 - core)
    right = along(lax.rem(z_lo + 1, 8))
    left = along(lax.rem(z_lo + 7, 8))

    def swap_blocks(src, dst):
        for half in range(2):
            lanes = pl.ds(half * LANES, LANES)
            turn[half] = src[:, lanes].astype(F32)
        for j in range(16):
            for half in range(2):
                block = turn[half, pl.ds(j, 16, stride=16), :]
                dst[pl.ds(16 * j, 16), pl.ds(half * LANES, LANES)] = block.astype(BF16)

    def swap_half(src, dst, half):
        turn[half] = src[half].astype(F32)
        for j in range(16):
            dst[half, pl.ds(16 * j, 16), :] = turn[half, pl.ds(j, 16, stride=16), :].astype(BF16)

    loads = [
        pltpu.make_async_copy(feat_hbm, feat, load_sem.at[0]),
        pltpu.make_async_copy(filt_hbm, filt, load_sem.at[1]),
        pltpu.make_async_copy(w_hbm, w, load_sem.at[2]),
        pltpu.make_async_copy(taps_hbm, taps, load_sem.at[3]),
        pltpu.make_async_copy(bias_hbm, bias_out, load_sem.at[4]),
    ]
    for which in (1, 0, 3, 4, 2):
        loads[which].start()

    barrier = pltpu.get_barrier_semaphore()
    peers = [across(lax.rem(z_hi + step, 4)) for step in (2, 1, 3, 0)]
    peers += [before]
    peers += [along(lax.rem(z_lo + step, 8)) for step in range(1, 8)]
    peers += [plane(step)[1] for step in range(1, 16)]
    peers += [sibling]
    for peer in peers:
        pl.semaphore_signal(barrier, inc=1, device_id=peer, device_id_type=MESH)

    loads[1].wait()
    swap_blocks(filt, filt_pre)
    for which in (0, 3, 4):
        loads[which].wait()

    row = lax.broadcasted_iota(jnp.int32, (16, SIDE), 0)
    pos = lax.broadcasted_iota(jnp.int32, (16, SIDE), 1)
    edge = jnp.zeros((16, SIDE), F32)
    for stream in range(3):
        pick = ((row - 2 * stream == pos - (SIDE - 2)) & (pos >= SIDE - 2)).astype(F32).astype(BF16)
        edge = edge + lax.dot_general(
            pick, feat[stream], (((1,), (1,)), ((), ())), preferred_element_type=F32
        )
    halo_out[...] = edge.astype(BF16)
    cols[...] = jnp.zeros((LANES, SIDE), F32)
    for stream in range(3):
        for tap in range(3):
            cols[pl.ds(3 * stream + tap, 1), :] = taps[stream, pl.ds(tap, 1), :]
    hpad[:, 0:8, :] = jnp.zeros((4, 8, LANES), F32)
    xpad[:, 0:8, :] = jnp.zeros((4, 8, LANES), F32)
    pairs[0:32, :] = jnp.zeros((32, LANES), F32)
    sums[0:32, :] = jnp.zeros((32, LANES), F32)

    lane = lax.broadcasted_iota(jnp.int32, (64, SIDE), 1)

    def shape(half, halo):
        turned = cols[...].T
        part = slice(half * LANES, (half + 1) * LANES)
        for block in range(4):
            rows = slice(64 * block, 64 * block + 64)
            shaped = []
            for stream in range(3):
                now = feat[stream, rows, :].astype(F32)
                one = pltpu.roll(now, 1, 1)
                two = pltpu.roll(now, 2, 1)
                if halo:
                    last = turned[rows, 16 + 2 * stream + 1 : 16 + 2 * stream + 2]
                    older = turned[rows, 16 + 2 * stream : 16 + 2 * stream + 1]
                    one = jnp.where(lane == 0, last, one)
                    two = jnp.where(lane == 0, older, jnp.where(lane == 1, last, two))
                tap = [turned[rows, 3 * stream + j : 3 * stream + j + 1] for j in range(3)]
                shaped.append(
                    tap[0] * now[:, part] + tap[1] * one[:, part] + tap[2] * two[:, part]
                )
            gate[rows, part] = shaped[0].astype(BF16)
            kv[half, rows, :] = (shaped[1] * shaped[2]).astype(BF16)

    shape(1, False)

    pl.semaphore_wait(barrier, len(peers))

    sent = []
    halo_copy = remote(halo_out, halo_in, halo_sem.at[0], halo_sem.at[1], after)
    halo_copy.start()
    bias_copy = remote(bias_out, bias_in, bias_sem.at[0], bias_sem.at[1], across(z_hi))
    bias_copy.start()

    sent.extend([halo_copy, bias_copy])

    def plane_exchange(src, dst, which):
        copies = []
        for step in range(1, 16):
            to, device = plane(step)
            copy = remote(
                src.at[pl.ds(pl.multiple_of(to * 16, 16), 16)],
                dst.at[pl.ds(pl.multiple_of(here * 16, 16), 16)],
                xy_send.at[which, step], xy_recv.at[which, step], device,
            )
            copy.start()
            copies.append(copy)
        mine = pl.ds(pl.multiple_of(here * 16, 16), 16)
        dst[mine, :] = src[mine, :]
        sent.extend(copies)
        return copies

    def across_exchange(src, dst, send, recv, first, rows):
        copies = []
        for step in (2, 1, 3, 0):
            to = lax.rem(z_hi + step, 4)
            copy = remote(
                src.at[pl.ds(pl.multiple_of(to * 64 + first, 16), rows)],
                dst.at[pl.ds(pl.multiple_of(z_hi * 64 + first, 16), rows)],
                send.at[step], recv.at[step], across(to),
            )
            copy.start()
            copies.append(copy)
        sent.extend(copies)
        return copies

    def arrived(copies):
        for copy in copies:
            copy.wait_recv()

    def spread(tile_of, dst, start, ch):
        for zs in range(4):
            for half in range(2):
                tile = tile_of(half, pl.ds(zs * 64 + ch * 16, 16)).astype(F32)
                for xs in range(4):
                    first = start + (xs * 16 + zs * 4) * 2 + half
                    dst[ch, pl.ds(first, 4, stride=2), :] = tile[4 * xs : 4 * xs + 4, :]

    filt_across = across_exchange(filt_pre, filt_zr, z_send, z_recv, 0, 64)

    kv_plane = plane_exchange(kv.at[1], kv_xy.at[1], 1)
    arrived(kv_plane)
    swap_half(kv_xy, kv_zs, 1)
    kv_across = across_exchange(
        kv_zs.at[1], kv_zr.at[1], kv_send.at[1], kv_recv.at[1], 0, 64
    )

    halo_copy.wait_recv()
    seen = jnp.where(context > 0, 1.0, 0.0)
    cols[16:32, :] = halo_in[...].astype(F32) * seen
    shape(0, True)
    kv_plane = plane_exchange(kv.at[0], kv_xy.at[0], 3)
    arrived(kv_plane)
    swap_half(kv_xy, kv_zs, 0)
    kv_across += across_exchange(
        kv_zs.at[0], kv_zr.at[0], kv_send.at[0], kv_recv.at[0], 0, 64
    )

    arrived(filt_across)
    swap_blocks(filt_zr, filt_zs)
    arrived(plane_exchange(filt_zs, filt_xy, 0))
    swap_blocks(filt_xy, filt_all)
    for ch in range(4):
        spread(lambda half, rows: filt_all[rows, pl.ds(half * LANES, LANES)], hpad, 8, ch)

    low = lax.broadcasted_iota(jnp.int32, (16, LANES), 1) < 64
    for ch in range(4):
        for a in range(4):
            one = hpad[ch, pl.ds(8 + 32 * a, 16), :]
            two = hpad[ch, pl.ds(24 + 32 * a, 16), :]
            even = jnp.where(low, one, pltpu.roll(two, 64, 1))
            odd = jnp.where(low, pltpu.roll(one, 64, 1), two)
            ahead[ch, pl.ds(32 * a, 16, stride=2), :] = even
            ahead[ch, pl.ds(32 * a + 1, 16, stride=2), :] = odd
            behind[ch, pl.ds(32 * a + 1, 16, stride=2), :] = pltpu.roll(even, 64, 1)
            behind[ch, pl.ds(32 * a + 2, 16, stride=2), :] = pltpu.roll(odd, 64, 1)
        for a in range(4):
            one = hpad[ch, pl.ds(23 + 32 * a, 1), :]
            two = hpad[ch, pl.ds(7 + 32 * a, 1), :]
            behind[ch, pl.ds(32 * a, 1), :] = jnp.where(low[:1], pltpu.roll(one, 64, 1), two)
    lane = lax.broadcasted_iota(jnp.int32, (64, LANES), 1)
    down = lax.broadcasted_iota(jnp.int32, (64, LANES), 0)
    keep = lax.rem(lane, 64) + down < 64

    def build(index, carry):
        ch = lax.div(index, 32)
        b = lax.rem(index, 32)
        for a in range(4):
            block = jnp.where(
                keep,
                jnp.broadcast_to(ahead[ch, pl.ds(32 * a + b, 1), :], (64, LANES)),
                jnp.broadcast_to(behind[ch, pl.ds(32 * a + b, 1), :], (64, LANES)),
            )
            block = pltpu.roll(block, 0, 1, stride=1, stride_axis=0)
            toep[ch, pl.ds(pl.multiple_of(b * 64, 64), 64), pl.ds(a * LANES, LANES)] = (
                block.astype(BF16)
            )
        return carry

    lax.fori_loop(0, 128, build, 0)

    bias_copy.wait_recv()
    spot = lax.broadcasted_iota(jnp.int32, (1, SIDE), 1)
    first_lanes = lax.broadcasted_iota(jnp.int32, (LANES, LANES), 1) < 64
    arrived(kv_across)
    back = []
    for ch in range(4):
        spread(lambda half, rows: kv_zr[half, rows, :], xpad, 8, ch)
        own_row = xpad[ch, pl.ds(8, LANES), :]
        row_before = xpad[ch, pl.ds(7, LANES), :]
        pairs[pl.ds(32, LANES, stride=2), :] = jnp.where(first_lanes, own_row, row_before)
        pairs[pl.ds(33, LANES, stride=2), :] = pltpu.roll(own_row, 64, 1)
        for b in range(16):
            xs_buf[:, pl.ds(b * LANES, LANES)] = pairs[pl.ds(32 - 2 * b, SIDE), :].astype(BF16)
        upper = jnp.dot(xs_buf[...], toep[ch, :, pl.ds(0, SIDE)], preferred_element_type=F32)
        lower = jnp.dot(
            xs_buf[pl.ds(0, LANES), :], toep[ch, :, pl.ds(SIDE, SIDE)],
            preferred_element_type=F32,
        )
        sums[pl.ds(32, SIDE), :] = upper[:, :LANES]
        sums[pl.ds(96, 192), :] += upper[:192, LANES:]
        sums[pl.ds(160, LANES), :] += lower[:, :LANES]
        sums[pl.ds(224, 64), :] += lower[:64, LANES:]
        folded[...] = sums[pl.ds(32, SIDE), :] + pltpu.roll(sums[pl.ds(0, SIDE), :], 64, 1)
        total = jnp.where(
            first_lanes,
            folded[pl.ds(0, LANES, stride=2), :],
            pltpu.roll(folded[pl.ds(1, LANES, stride=2), :], 64, 1),
        )
        channel = here * 16 + z_hi * 4 + ch
        bias = jnp.sum(jnp.where(spot == channel, bias_in[...], 0.0), axis=1, keepdims=True)
        ypad[...] = total + bias * own_row
        for zs in range(4):
            for xs in range(4):
                for half in range(2):
                    first = (xs * 16 + zs * 4) * 2 + half
                    piece[pl.ds(4 * xs, 4), pl.ds(half * LANES, LANES)] = ypad[
                        pl.ds(first, 4, stride=2), :
                    ]
            mix_zs[pl.ds(zs * 64 + ch * 16, 16), :] = piece[...].astype(BF16)
        if ch % 2:
            group = ch // 2
            back += across_exchange(
                mix_zs, mix_zr, back_send.at[group], back_recv.at[group], 32 * group, 32
            )

    arrived(back)
    swap_blocks(mix_zr, mix_ss)
    arrived(plane_exchange(mix_ss, mix, 2))

    gated = (gate[...].astype(F32) * mix[...].astype(F32)).astype(BF16).astype(F32)
    gated_t[...] = gated.T.astype(BF16)
    loads[2].wait()

    def sib_copy(d):
        return remote(sib_out.at[d], sib_in.at[d], sib_send.at[d], sib_recv.at[d], sibling)

    for d in (7, 0, 6, 1, 5, 2, 4, 3):
        theirs = pl.ds(pl.multiple_of((2 * d + 1 - core) * SIDE, SIDE), SIDE)
        mine = pl.ds(pl.multiple_of((2 * d + core) * SIDE, SIDE), SIDE)
        sib_out[d] = jnp.dot(gated_t[...], w[:, theirs], preferred_element_type=F32).astype(BF16)
        sib_copy(d).start()
        own[d] = jnp.dot(gated_t[...], w[:, mine], preferred_element_type=F32)

    size = SIDE // PARTS

    def rows_of(n):
        return pl.ds(pl.multiple_of(lax.rem(n, PARTS) * size, size), size)

    quarter = lax.rem(z_lo, 4)

    def right_copy(n):
        d = 7 - lax.div(n, PARTS)
        return remote(
            right_out.at[d, rows_of(n)], right_in.at[d, rows_of(n)],
            right_send.at[n], right_recv.at[n], right,
        )

    def right_jump(n, d):
        return remote(
            right_out.at[7 - lax.div(n, PARTS), rows_of(n)], right_far.at[rows_of(n)],
            right_send.at[n], right_recv.at[STEPS + lax.rem(n, PARTS)], along(d),
        )

    def left_copy(n):
        d = lax.div(n, PARTS)
        return remote(
            left_out.at[d, rows_of(n)], left_in.at[d, rows_of(n)],
            left_send.at[n], left_recv.at[n], left,
        )

    def left_jump(n, d):
        return remote(
            left_out.at[lax.div(n, PARTS), rows_of(n)], left_far.at[rows_of(n)],
            left_send.at[n], left_recv.at[STEPS + lax.rem(n, PARTS)], along(d),
        )

    def pass_on(n, d, first, jumps, copy, jump, came, going):
        rows = rows_of(n)

        @pl.when(lax.rem(n, PARTS) == 0)
        def _():
            sib_copy(d).wait_recv()

        @pl.when(first)
        def _():
            going[d, rows, :] = (own[d, rows, :] + sib_in[d, rows, :].astype(F32)).astype(BF16)

        @pl.when(jnp.logical_not(first))
        def _():
            copy.wait_recv()
            going[d, rows, :] = (
                own[d, rows, :] + sib_in[d, rows, :].astype(F32) + came[d, rows, :].astype(F32)
            ).astype(BF16)

        @pl.when(jumps)
        def _():
            jump.start()

        @pl.when(jnp.logical_not(jumps))
        def _():
            copy.start()

    def reduce_step(moment, carry):
        n = moment - quarter * LAG

        @pl.when((n >= 0) & (n < (7 - z_lo) * PARTS))
        def _():
            d = 7 - lax.div(n, PARTS)
            pass_on(
                n, d, quarter == 0, (z_lo == 3) & (d > 4),
                right_copy(n), right_jump(n, d), right_in, right_out,
            )

        m = moment - (3 - quarter) * LAG

        @pl.when((m >= 0) & (m < z_lo * PARTS))
        def _():
            d = lax.div(m, PARTS)
            pass_on(
                m, d, quarter == 3, (z_lo == 4) & (d < 3),
                left_copy(m), left_jump(m, d), left_in, left_out,
            )

        return carry

    lax.fori_loop(0, STEPS + 3 * LAG, reduce_step, 0)

    sib_copy(z_lo).wait_recv()
    own[z_lo] = own[z_lo] + sib_in[z_lo].astype(F32)

    @pl.when(z_lo > 0)
    def _():
        for part in range(PARTS):
            right_copy((7 - z_lo) * PARTS + part).wait_recv()
        own[z_lo] = own[z_lo] + right_in[z_lo].astype(F32)

    @pl.when(z_lo < 7)
    def _():
        for part in range(PARTS):
            left_copy(z_lo * PARTS + part).wait_recv()
        own[z_lo] = own[z_lo] + left_in[z_lo].astype(F32)

    @pl.when(z_lo > 4)
    def _():
        for part in range(PARTS):
            right_jump(part, z_lo).wait_recv()
        own[z_lo] = own[z_lo] + right_far[...].astype(F32)

    @pl.when(z_lo < 3)
    def _():
        for part in range(PARTS):
            left_jump(part, z_lo).wait_recv()
        own[z_lo] = own[z_lo] + left_far[...].astype(F32)

    out_ref[...] = own[z_lo].astype(BF16)

    for copy in sent:
        copy.wait_send()
    for d in range(8):
        sib_copy(d).wait_send()

    def close(n, carry):
        @pl.when(n < (7 - z_lo) * PARTS)
        def _():
            right_copy(n).wait_send()

        @pl.when(n < z_lo * PARTS)
        def _():
            left_copy(n).wait_send()

        return carry

    lax.fori_loop(0, STEPS, close, 0)


def local(features, short_taps, long_filter, skip_bias, out_weight):
    vmem = pl.BlockSpec(memory_space=pltpu.VMEM)
    anywhere = pl.BlockSpec(memory_space=pl.ANY)
    square = pltpu.VMEM((SIDE, SIDE), BF16)
    halves = pltpu.VMEM((2, SIDE, LANES), BF16)
    dma = pltpu.SemaphoreType.DMA
    return pl.pallas_call(
        kernel,
        out_shape=jax.ShapeDtypeStruct((SIDE, SIDE), BF16),
        in_specs=[anywhere] * 5,
        out_specs=vmem,
        scratch_shapes=[
            pltpu.VMEM((3, SIDE, SIDE), BF16),
            pltpu.VMEM((3, 3, SIDE), F32),
            square,
            pltpu.VMEM((1, SIDE), F32),
            pltpu.VMEM((SIDE, 16 * SIDE), BF16),
            pltpu.VMEM((LANES, SIDE), F32),
            pltpu.VMEM((16, SIDE), BF16),
            pltpu.VMEM((16, SIDE), BF16),
            pltpu.VMEM((1, SIDE), F32),
            square, halves,
            square, square, square, square, square,
            halves, halves, halves,
            square, square, square, square,
            pltpu.VMEM((2, SIDE, LANES), F32),
            pltpu.VMEM((4, 136, LANES), F32),
            pltpu.VMEM((4, LANES, LANES), F32),
            pltpu.VMEM((4, 136, LANES), F32),
            pltpu.VMEM((4, 136, LANES), F32),
            pltpu.VMEM((32 + SIDE, LANES), F32),
            pltpu.VMEM((32 + SIDE, LANES), F32),
            pltpu.VMEM((SIDE, LANES), F32),
            pltpu.VMEM((LANES, LANES), F32),
            pltpu.VMEM((16, SIDE), F32),
            pltpu.VMEM((SIDE, 2048), BF16),
            pltpu.VMEM((4, 2048, 512), BF16),
            square,
            pltpu.VMEM((8, SIDE, SIDE), BF16),
            pltpu.VMEM((8, SIDE, SIDE), BF16),
            pltpu.VMEM((8, SIDE, SIDE), F32),
            pltpu.VMEM((8, SIDE, SIDE), BF16), pltpu.VMEM((8, SIDE, SIDE), BF16), square,
            pltpu.VMEM((8, SIDE, SIDE), BF16), pltpu.VMEM((8, SIDE, SIDE), BF16), square,
            dma((5,)), dma((2,)), dma((2,)),
            dma((4, 16)), dma((4, 16)),
            dma((4,)), dma((4,)),
            dma((2, 4)), dma((2, 4)),
            dma((2, 4)), dma((2, 4)),
            dma((8,)), dma((8,)),
            dma((STEPS,)), dma((STEPS + PARTS,)), dma((STEPS,)), dma((STEPS + PARTS,)),
        ],
        compiler_params=pltpu.CompilerParams(
            collective_id=0, has_side_effects=True, vmem_limit_bytes=60 << 20
        ),
        cost_estimate=pl.CostEstimate(
            flops=4 * 10**9, bytes_accessed=3 * 10**6, transcendentals=0
        ),
        name="hyena_operator",
    )(features, short_taps, long_filter, skip_bias.reshape(1, SIDE), out_weight)


def solution(mesh):
    placed = (
        P(None, "tensor", "context"),
        P(None, None, "tensor"),
        P("tensor", "context"),
        P("tensor"),
        P("tensor", None),
    )
    return jax.shard_map(
        local, mesh=mesh, in_specs=placed, out_specs=P("context", "tensor"), check_vma=False
    )
```

```python
import jax
import jax.numpy as jnp
from jax import lax
from jax.experimental import pallas as pl
from jax.experimental.pallas import tpu as pltpu
from jax.sharding import PartitionSpec as P

MESH = pl.DeviceIdType.MESH
F32 = jnp.float32
BF16 = jnp.bfloat16
SIDE = 256
LANES = 128
PARTS = 4
LAG = 4
STEPS = 7 * PARTS
PLACES = (10, 9, 11, 6, 14, 2, 8, 5, 7, 13, 15, 1, 3, 4, 12)


def remote(src, dst, send_sem, recv_sem, device):
    return pltpu.make_async_remote_copy(
        src_ref=src, dst_ref=dst, send_sem=send_sem, recv_sem=recv_sem,
        device_id=device, device_id_type=MESH,
    )


def kernel(
    feat_hbm, taps_hbm, filt_hbm, bias_hbm, w_hbm, out_ref,
    feat, taps, filt, bias_out, w, cols, halo_out, halo_in, bias_in, gate, kv,
    filt_pre, filt_zr, filt_zs, filt_xy, filt_all, kv_xy, kv_zs, kv_zr,
    mix_zs, mix_zr, mix_ss, mix,
    turn, hpad, ahead, behind, xpad, pairs, sums, folded, ypad, piece, xs_buf, toep, gated_t,
    sib_out, sib_in, own, right_out, right_in, right_far, left_out, left_in, left_far,
    load_sem, halo_sem, bias_sem,
    xy_send, xy_recv, z_send, z_recv, kv_send, kv_recv, back_send, back_recv,
    sib_send, sib_recv, right_send, right_recv, left_send, left_recv,
):
    context = lax.axis_index("context")
    tensor = lax.axis_index("tensor")
    x = lax.div(context, 16)
    y = lax.rem(context, 4)
    z_hi = lax.rem(lax.div(context, 4), 4)
    z_lo = lax.div(tensor, 2)
    core = lax.rem(tensor, 2)
    here = x * 4 + y

    def plane(step):
        to_x = lax.rem(x + step // 4, 4)
        to_y = lax.rem(y + step % 4, 4)
        return to_x * 4 + to_y, (to_x * 16 + z_hi * 4 + to_y, tensor)

    opposite = lax.rem(z_lo + 4, 8) * 2 + core

    def across(target_hi):
        return (x * 16 + target_hi * 4 + y, opposite)

    def along(target_lo):
        return (context, target_lo * 2 + core)

    after = (lax.rem(context + 1, 64), tensor)
    before = (lax.rem(context + 63, 64), tensor)
    sibling = (context, z_lo * 2 + 1 - core)
    right = along(lax.rem(z_lo + 1, 8))
    left = along(lax.rem(z_lo + 7, 8))

    def swap_blocks(src, dst):
        for half in range(2):
            lanes = pl.ds(half * LANES, LANES)
            turn[half] = src[:, lanes].astype(F32)
        for j in range(16):
            for half in range(2):
                block = turn[half, pl.ds(j, 16, stride=16), :]
                dst[pl.ds(16 * j, 16), pl.ds(half * LANES, LANES)] = block.astype(BF16)

    loads = [
        pltpu.make_async_copy(feat_hbm, feat, load_sem.at[0]),
        pltpu.make_async_copy(filt_hbm, filt, load_sem.at[1]),
        pltpu.make_async_copy(w_hbm, w, load_sem.at[2]),
        pltpu.make_async_copy(taps_hbm, taps, load_sem.at[3]),
        pltpu.make_async_copy(bias_hbm, bias_out, load_sem.at[4]),
    ]
    for which in (1, 0, 3, 4, 2):
        loads[which].start()

    barrier = pltpu.get_barrier_semaphore()
    peers = [across(lax.rem(z_hi + step, 4)) for step in (2, 1, 3, 0)]
    peers += [before]
    peers += [along(lax.rem(z_lo + step, 8)) for step in range(1, 8)]
    peers += [plane(step)[1] for step in PLACES]
    peers += [sibling]
    for peer in peers:
        pl.semaphore_signal(barrier, inc=1, device_id=peer, device_id_type=MESH)

    loads[1].wait()
    swap_blocks(filt, filt_pre)
    for which in (0, 3, 4):
        loads[which].wait()

    row = lax.broadcasted_iota(jnp.int32, (16, SIDE), 0)
    pos = lax.broadcasted_iota(jnp.int32, (16, SIDE), 1)
    edge = jnp.zeros((16, SIDE), F32)
    for stream in range(3):
        pick = ((row - 2 * stream == pos - (SIDE - 2)) & (pos >= SIDE - 2)).astype(F32).astype(BF16)
        edge = edge + lax.dot_general(
            pick, feat[stream], (((1,), (1,)), ((), ())), preferred_element_type=F32
        )
    halo_out[...] = edge.astype(BF16)
    cols[...] = jnp.zeros((LANES, SIDE), F32)
    for stream in range(3):
        for tap in range(3):
            cols[pl.ds(3 * stream + tap, 1), :] = taps[stream, pl.ds(tap, 1), :]
    hpad[:, 0:8, :] = jnp.zeros((4, 8, LANES), F32)
    xpad[:, 0:8, :] = jnp.zeros((4, 8, LANES), F32)
    pairs[0:32, :] = jnp.zeros((32, LANES), F32)
    sums[0:32, :] = jnp.zeros((32, LANES), F32)

    lane = lax.broadcasted_iota(jnp.int32, (64, SIDE), 1)

    def shape(half, halo):
        turned = cols[...].T
        part = slice(half * LANES, (half + 1) * LANES)
        for block in range(4):
            rows = slice(64 * block, 64 * block + 64)
            shaped = []
            for stream in range(3):
                now = feat[stream, rows, :].astype(F32)
                one = pltpu.roll(now, 1, 1)
                two = pltpu.roll(now, 2, 1)
                if halo:
                    last = turned[rows, 16 + 2 * stream + 1 : 16 + 2 * stream + 2]
                    older = turned[rows, 16 + 2 * stream : 16 + 2 * stream + 1]
                    one = jnp.where(lane == 0, last, one)
                    two = jnp.where(lane == 0, older, jnp.where(lane == 1, last, two))
                tap = [turned[rows, 3 * stream + j : 3 * stream + j + 1] for j in range(3)]
                shaped.append(
                    tap[0] * now[:, part] + tap[1] * one[:, part] + tap[2] * two[:, part]
                )
            gate[rows, part] = shaped[0].astype(BF16)
            kv[rows, part] = (shaped[1] * shaped[2]).astype(BF16)

    shape(1, False)

    pl.semaphore_wait(barrier, len(peers))

    sent = []
    halo_copy = remote(halo_out, halo_in, halo_sem.at[0], halo_sem.at[1], after)
    halo_copy.start()
    bias_copy = remote(bias_out, bias_in, bias_sem.at[0], bias_sem.at[1], across(z_hi))
    bias_copy.start()

    sent.extend([halo_copy, bias_copy])

    def plane_exchange(src, dst, which):
        copies = []
        for step in PLACES:
            to, device = plane(step)
            copy = remote(
                src.at[pl.ds(pl.multiple_of(to * 16, 16), 16)],
                dst.at[pl.ds(pl.multiple_of(here * 16, 16), 16)],
                xy_send.at[which, step], xy_recv.at[which, step], device,
            )
            copy.start()
            copies.append(copy)
        mine = pl.ds(pl.multiple_of(here * 16, 16), 16)
        dst[mine, :] = src[mine, :]
        sent.extend(copies)
        return copies

    def across_exchange(src, dst, send, recv, first, rows):
        copies = []
        for step in (2, 1, 3, 0):
            to = lax.rem(z_hi + step, 4)
            copy = remote(
                src.at[pl.ds(pl.multiple_of(to * 64 + first, 16), rows)],
                dst.at[pl.ds(pl.multiple_of(z_hi * 64 + first, 16), rows)],
                send.at[step], recv.at[step], across(to),
            )
            copy.start()
            copies.append(copy)
        sent.extend(copies)
        return copies

    def arrived(copies):
        for copy in copies:
            copy.wait_recv()

    def spread(src, dst, start, ch):
        for zs in range(4):
            tile = src[pl.ds(zs * 64 + ch * 16, 16), :].astype(F32)
            for xs in range(4):
                for half in range(2):
                    first = start + (xs * 16 + zs * 4) * 2 + half
                    dst[ch, pl.ds(first, 4, stride=2), :] = tile[
                        4 * xs : 4 * xs + 4, half * LANES : (half + 1) * LANES
                    ]

    filt_across = across_exchange(filt_pre, filt_zr, z_send, z_recv, 0, 64)

    halo_copy.wait_recv()
    seen = jnp.where(context > 0, 1.0, 0.0)
    cols[16:32, :] = halo_in[...].astype(F32) * seen
    shape(0, True)

    kv_plane = plane_exchange(kv, kv_xy, 1)
    arrived(kv_plane)
    swap_blocks(kv_xy, kv_zs)
    kv_across = [
        across_exchange(kv_zs, kv_zr, kv_send.at[ch], kv_recv.at[ch], 16 * ch, 16)
        for ch in range(4)
    ]

    arrived(filt_across)
    swap_blocks(filt_zr, filt_zs)
    arrived(plane_exchange(filt_zs, filt_xy, 0))
    swap_blocks(filt_xy, filt_all)
    for ch in range(4):
        spread(filt_all, hpad, 8, ch)

    low = lax.broadcasted_iota(jnp.int32, (16, LANES), 1) < 64
    for ch in range(4):
        for a in range(4):
            one = hpad[ch, pl.ds(8 + 32 * a, 16), :]
            two = hpad[ch, pl.ds(24 + 32 * a, 16), :]
            even = jnp.where(low, one, pltpu.roll(two, 64, 1))
            odd = jnp.where(low, pltpu.roll(one, 64, 1), two)
            ahead[ch, pl.ds(32 * a, 16, stride=2), :] = even
            ahead[ch, pl.ds(32 * a + 1, 16, stride=2), :] = odd
            behind[ch, pl.ds(32 * a + 1, 16, stride=2), :] = pltpu.roll(even, 64, 1)
            behind[ch, pl.ds(32 * a + 2, 16, stride=2), :] = pltpu.roll(odd, 64, 1)
        for a in range(4):
            one = hpad[ch, pl.ds(23 + 32 * a, 1), :]
            two = hpad[ch, pl.ds(7 + 32 * a, 1), :]
            behind[ch, pl.ds(32 * a, 1), :] = jnp.where(low[:1], pltpu.roll(one, 64, 1), two)
    lane = lax.broadcasted_iota(jnp.int32, (64, LANES), 1)
    down = lax.broadcasted_iota(jnp.int32, (64, LANES), 0)
    keep = lax.rem(lane, 64) + down < 64

    def build(index, carry):
        ch = lax.div(index, 32)
        b = lax.rem(index, 32)
        for a in range(4):
            block = jnp.where(
                keep,
                jnp.broadcast_to(ahead[ch, pl.ds(32 * a + b, 1), :], (64, LANES)),
                jnp.broadcast_to(behind[ch, pl.ds(32 * a + b, 1), :], (64, LANES)),
            )
            block = pltpu.roll(block, 0, 1, stride=1, stride_axis=0)
            toep[ch, pl.ds(pl.multiple_of(b * 64, 64), 64), pl.ds(a * LANES, LANES)] = (
                block.astype(BF16)
            )
        return carry

    lax.fori_loop(0, 128, build, 0)

    bias_copy.wait_recv()
    spot = lax.broadcasted_iota(jnp.int32, (1, SIDE), 1)
    first_lanes = lax.broadcasted_iota(jnp.int32, (LANES, LANES), 1) < 64
    back = []
    for ch in range(4):
        arrived(kv_across[ch])
        spread(kv_zr, xpad, 8, ch)
        own_row = xpad[ch, pl.ds(8, LANES), :]
        row_before = xpad[ch, pl.ds(7, LANES), :]
        pairs[pl.ds(32, LANES, stride=2), :] = jnp.where(first_lanes, own_row, row_before)
        pairs[pl.ds(33, LANES, stride=2), :] = pltpu.roll(own_row, 64, 1)
        for b in range(16):
            xs_buf[:, pl.ds(b * LANES, LANES)] = pairs[pl.ds(32 - 2 * b, SIDE), :].astype(BF16)
        upper = jnp.dot(xs_buf[...], toep[ch, :, pl.ds(0, SIDE)], preferred_element_type=F32)
        lower = jnp.dot(
            xs_buf[pl.ds(0, LANES), :], toep[ch, :, pl.ds(SIDE, SIDE)],
            preferred_element_type=F32,
        )
        sums[pl.ds(32, SIDE), :] = upper[:, :LANES]
        sums[pl.ds(96, 192), :] += upper[:192, LANES:]
        sums[pl.ds(160, LANES), :] += lower[:, :LANES]
        sums[pl.ds(224, 64), :] += lower[:64, LANES:]
        folded[...] = sums[pl.ds(32, SIDE), :] + pltpu.roll(sums[pl.ds(0, SIDE), :], 64, 1)
        total = jnp.where(
            first_lanes,
            folded[pl.ds(0, LANES, stride=2), :],
            pltpu.roll(folded[pl.ds(1, LANES, stride=2), :], 64, 1),
        )
        channel = here * 16 + z_hi * 4 + ch
        bias = jnp.sum(jnp.where(spot == channel, bias_in[...], 0.0), axis=1, keepdims=True)
        ypad[...] = total + bias * own_row
        for zs in range(4):
            for xs in range(4):
                for half in range(2):
                    first = (xs * 16 + zs * 4) * 2 + half
                    piece[pl.ds(4 * xs, 4), pl.ds(half * LANES, LANES)] = ypad[
                        pl.ds(first, 4, stride=2), :
                    ]
            mix_zs[pl.ds(zs * 64 + ch * 16, 16), :] = piece[...].astype(BF16)
        back += across_exchange(
            mix_zs, mix_zr, back_send.at[ch], back_recv.at[ch], 16 * ch, 16
        )

    arrived(back)
    swap_blocks(mix_zr, mix_ss)
    arrived(plane_exchange(mix_ss, mix, 2))

    gated = (gate[...].astype(F32) * mix[...].astype(F32)).astype(BF16).astype(F32)
    gated_t[...] = gated.T.astype(BF16)
    loads[2].wait()

    def sib_copy(d):
        return remote(sib_out.at[d], sib_in.at[d], sib_send.at[d], sib_recv.at[d], sibling)

    for d in (7, 0, 6, 1, 5, 2, 4, 3):
        theirs = pl.ds(pl.multiple_of((2 * d + 1 - core) * SIDE, SIDE), SIDE)
        mine = pl.ds(pl.multiple_of((2 * d + core) * SIDE, SIDE), SIDE)
        sib_out[d] = jnp.dot(gated_t[...], w[:, theirs], preferred_element_type=F32).astype(BF16)
        sib_copy(d).start()
        own[d] = jnp.dot(gated_t[...], w[:, mine], preferred_element_type=F32)

    size = SIDE // PARTS

    def rows_of(n):
        return pl.ds(pl.multiple_of(lax.rem(n, PARTS) * size, size), size)

    quarter = lax.rem(z_lo, 4)

    def right_copy(n):
        d = 7 - lax.div(n, PARTS)
        return remote(
            right_out.at[d, rows_of(n)], right_in.at[d, rows_of(n)],
            right_send.at[n], right_recv.at[n], right,
        )

    def right_jump(n, d):
        return remote(
            right_out.at[7 - lax.div(n, PARTS), rows_of(n)], right_far.at[rows_of(n)],
            right_send.at[n], right_recv.at[STEPS + lax.rem(n, PARTS)], along(d),
        )

    def left_copy(n):
        d = lax.div(n, PARTS)
        return remote(
            left_out.at[d, rows_of(n)], left_in.at[d, rows_of(n)],
            left_send.at[n], left_recv.at[n], left,
        )

    def left_jump(n, d):
        return remote(
            left_out.at[lax.div(n, PARTS), rows_of(n)], left_far.at[rows_of(n)],
            left_send.at[n], left_recv.at[STEPS + lax.rem(n, PARTS)], along(d),
        )

    def pass_on(n, d, first, jumps, copy, jump, came, going):
        rows = rows_of(n)

        @pl.when(lax.rem(n, PARTS) == 0)
        def _():
            sib_copy(d).wait_recv()

        @pl.when(first)
        def _():
            going[d, rows, :] = (own[d, rows, :] + sib_in[d, rows, :].astype(F32)).astype(BF16)

        @pl.when(jnp.logical_not(first))
        def _():
            copy.wait_recv()
            going[d, rows, :] = (
                own[d, rows, :] + sib_in[d, rows, :].astype(F32) + came[d, rows, :].astype(F32)
            ).astype(BF16)

        @pl.when(jumps)
        def _():
            jump.start()

        @pl.when(jnp.logical_not(jumps))
        def _():
            copy.start()

    def reduce_step(moment, carry):
        n = moment - quarter * LAG

        @pl.when((n >= 0) & (n < (7 - z_lo) * PARTS))
        def _():
            d = 7 - lax.div(n, PARTS)
            pass_on(
                n, d, quarter == 0, (z_lo == 3) & (d > 4),
                right_copy(n), right_jump(n, d), right_in, right_out,
            )

        m = moment - (3 - quarter) * LAG

        @pl.when((m >= 0) & (m < z_lo * PARTS))
        def _():
            d = lax.div(m, PARTS)
            pass_on(
                m, d, quarter == 3, (z_lo == 4) & (d < 3),
                left_copy(m), left_jump(m, d), left_in, left_out,
            )

        return carry

    lax.fori_loop(0, STEPS + 3 * LAG, reduce_step, 0)

    sib_copy(z_lo).wait_recv()
    own[z_lo] = own[z_lo] + sib_in[z_lo].astype(F32)

    @pl.when(z_lo > 0)
    def _():
        for part in range(PARTS):
            right_copy((7 - z_lo) * PARTS + part).wait_recv()
        own[z_lo] = own[z_lo] + right_in[z_lo].astype(F32)

    @pl.when(z_lo < 7)
    def _():
        for part in range(PARTS):
            left_copy(z_lo * PARTS + part).wait_recv()
        own[z_lo] = own[z_lo] + left_in[z_lo].astype(F32)

    @pl.when(z_lo > 4)
    def _():
        for part in range(PARTS):
            right_jump(part, z_lo).wait_recv()
        own[z_lo] = own[z_lo] + right_far[...].astype(F32)

    @pl.when(z_lo < 3)
    def _():
        for part in range(PARTS):
            left_jump(part, z_lo).wait_recv()
        own[z_lo] = own[z_lo] + left_far[...].astype(F32)

    out_ref[...] = own[z_lo].astype(BF16)

    for copy in sent:
        copy.wait_send()
    for d in range(8):
        sib_copy(d).wait_send()

    def close(n, carry):
        @pl.when(n < (7 - z_lo) * PARTS)
        def _():
            right_copy(n).wait_send()

        @pl.when(n < z_lo * PARTS)
        def _():
            left_copy(n).wait_send()

        return carry

    lax.fori_loop(0, STEPS, close, 0)


def local(features, short_taps, long_filter, skip_bias, out_weight):
    vmem = pl.BlockSpec(memory_space=pltpu.VMEM)
    anywhere = pl.BlockSpec(memory_space=pl.ANY)
    square = pltpu.VMEM((SIDE, SIDE), BF16)
    dma = pltpu.SemaphoreType.DMA
    return pl.pallas_call(
        kernel,
        out_shape=jax.ShapeDtypeStruct((SIDE, SIDE), BF16),
        in_specs=[anywhere] * 5,
        out_specs=vmem,
        scratch_shapes=[
            pltpu.VMEM((3, SIDE, SIDE), BF16),
            pltpu.VMEM((3, 3, SIDE), F32),
            square,
            pltpu.VMEM((1, SIDE), F32),
            pltpu.VMEM((SIDE, 16 * SIDE), BF16),
            pltpu.VMEM((LANES, SIDE), F32),
            pltpu.VMEM((16, SIDE), BF16),
            pltpu.VMEM((16, SIDE), BF16),
            pltpu.VMEM((1, SIDE), F32),
            square, square,
            square, square, square, square, square,
            square, square, square,
            square, square, square, square,
            pltpu.VMEM((2, SIDE, LANES), F32),
            pltpu.VMEM((4, 136, LANES), F32),
            pltpu.VMEM((4, LANES, LANES), F32),
            pltpu.VMEM((4, 136, LANES), F32),
            pltpu.VMEM((4, 136, LANES), F32),
            pltpu.VMEM((32 + SIDE, LANES), F32),
            pltpu.VMEM((32 + SIDE, LANES), F32),
            pltpu.VMEM((SIDE, LANES), F32),
            pltpu.VMEM((LANES, LANES), F32),
            pltpu.VMEM((16, SIDE), F32),
            pltpu.VMEM((SIDE, 2048), BF16),
            pltpu.VMEM((4, 2048, 512), BF16),
            square,
            pltpu.VMEM((8, SIDE, SIDE), BF16),
            pltpu.VMEM((8, SIDE, SIDE), BF16),
            pltpu.VMEM((8, SIDE, SIDE), F32),
            pltpu.VMEM((8, SIDE, SIDE), BF16), pltpu.VMEM((8, SIDE, SIDE), BF16), square,
            pltpu.VMEM((8, SIDE, SIDE), BF16), pltpu.VMEM((8, SIDE, SIDE), BF16), square,
            dma((5,)), dma((2,)), dma((2,)),
            dma((3, 16)), dma((3, 16)),
            dma((4,)), dma((4,)),
            dma((4, 4)), dma((4, 4)),
            dma((4, 4)), dma((4, 4)),
            dma((8,)), dma((8,)),
            dma((STEPS,)), dma((STEPS + PARTS,)), dma((STEPS,)), dma((STEPS + PARTS,)),
        ],
        compiler_params=pltpu.CompilerParams(
            collective_id=0, has_side_effects=True, vmem_limit_bytes=60 << 20
        ),
        cost_estimate=pl.CostEstimate(
            flops=4 * 10**9, bytes_accessed=3 * 10**6, transcendentals=0
        ),
        name="hyena_operator",
    )(features, short_taps, long_filter, skip_bias.reshape(1, SIDE), out_weight)


def solution(mesh):
    placed = (
        P(None, "tensor", "context"),
        P(None, None, "tensor"),
        P("tensor", "context"),
        P("tensor"),
        P("tensor", None),
    )
    return jax.shard_map(
        local, mesh=mesh, in_specs=placed, out_specs=P("context", "tensor"), check_vma=False
    )
```

```python
import jax
import jax.numpy as jnp
from jax import lax
from jax.experimental import pallas as pl
from jax.experimental.pallas import tpu as pltpu
from jax.sharding import PartitionSpec as P

MESH = pl.DeviceIdType.MESH
F32 = jnp.float32
BF16 = jnp.bfloat16
SIDE = 256
LANES = 128
PARTS = 4
LAG = 4
STEPS = 7 * PARTS
PLACES = (10, 9, 11, 6, 14, 2, 8, 5, 7, 13, 15, 1, 3, 4, 12)


def remote(src, dst, send_sem, recv_sem, device):
    return pltpu.make_async_remote_copy(
        src_ref=src, dst_ref=dst, send_sem=send_sem, recv_sem=recv_sem,
        device_id=device, device_id_type=MESH,
    )


def kernel(
    feat_hbm, taps_hbm, filt_hbm, bias_hbm, w_hbm, out_ref,
    feat, taps, filt, bias_out, w, cols, halo_out, halo_in, bias_in, gate, kv,
    filt_pre, filt_zr, filt_zs, filt_xy, filt_all, kv_xy, kv_zs, kv_zr,
    mix_zs, mix_zr, mix_ss, mix,
    turn, hpad, ahead, behind, xpad, pairs, sums, folded, ypad, piece, xs_buf, toep, gated_t,
    sib_out, sib_in, own, right_out, right_in, right_far, left_out, left_in, left_far,
    load_sem, halo_sem, bias_sem,
    xy_send, xy_recv, z_send, z_recv, kv_send, kv_recv, back_send, back_recv,
    sib_send, sib_recv, right_send, right_recv, left_send, left_recv,
):
    context = lax.axis_index("context")
    tensor = lax.axis_index("tensor")
    x = lax.div(context, 16)
    y = lax.rem(context, 4)
    z_hi = lax.rem(lax.div(context, 4), 4)
    z_lo = lax.div(tensor, 2)
    core = lax.rem(tensor, 2)
    here = x * 4 + y

    def plane(step):
        to_x = lax.rem(x + step // 4, 4)
        to_y = lax.rem(y + step % 4, 4)
        return to_x * 4 + to_y, (to_x * 16 + z_hi * 4 + to_y, tensor)

    opposite = lax.rem(z_lo + 4, 8) * 2 + core

    def across(target_hi):
        return (x * 16 + target_hi * 4 + y, opposite)

    def along(target_lo):
        return (context, target_lo * 2 + core)

    after = (lax.rem(context + 1, 64), tensor)
    before = (lax.rem(context + 63, 64), tensor)
    sibling = (context, z_lo * 2 + 1 - core)
    right = along(lax.rem(z_lo + 1, 8))
    left = along(lax.rem(z_lo + 7, 8))

    def swap_blocks(src, dst):
        for half in range(2):
            lanes = pl.ds(half * LANES, LANES)
            turn[half] = src[:, lanes].astype(F32)
        for j in range(16):
            for half in range(2):
                block = turn[half, pl.ds(j, 16, stride=16), :]
                dst[pl.ds(16 * j, 16), pl.ds(half * LANES, LANES)] = block.astype(BF16)

    loads = [
        pltpu.make_async_copy(feat_hbm, feat, load_sem.at[0]),
        pltpu.make_async_copy(filt_hbm, filt, load_sem.at[1]),
        pltpu.make_async_copy(w_hbm, w, load_sem.at[2]),
        pltpu.make_async_copy(taps_hbm, taps, load_sem.at[3]),
        pltpu.make_async_copy(bias_hbm, bias_out, load_sem.at[4]),
    ]
    for which in (1, 0, 3, 4, 2):
        loads[which].start()

    barrier = pltpu.get_barrier_semaphore()
    peers = [across(lax.rem(z_hi + step, 4)) for step in (2, 1, 3, 0)]
    peers += [before]
    peers += [along(lax.rem(z_lo + step, 8)) for step in range(1, 8)]
    peers += [plane(step)[1] for step in PLACES]
    peers += [sibling]
    for peer in peers:
        pl.semaphore_signal(barrier, inc=1, device_id=peer, device_id_type=MESH)

    loads[1].wait()
    swap_blocks(filt, filt_pre)
    for which in (0, 3, 4):
        loads[which].wait()

    row = lax.broadcasted_iota(jnp.int32, (16, SIDE), 0)
    pos = lax.broadcasted_iota(jnp.int32, (16, SIDE), 1)
    edge = jnp.zeros((16, SIDE), F32)
    for stream in range(3):
        pick = ((row - 2 * stream == pos - (SIDE - 2)) & (pos >= SIDE - 2)).astype(F32).astype(BF16)
        edge = edge + lax.dot_general(
            pick, feat[stream], (((1,), (1,)), ((), ())), preferred_element_type=F32
        )
    halo_out[...] = edge.astype(BF16)
    cols[...] = jnp.zeros((LANES, SIDE), F32)
    for stream in range(3):
        for tap in range(3):
            cols[pl.ds(3 * stream + tap, 1), :] = taps[stream, pl.ds(tap, 1), :]
    hpad[:, 0:8, :] = jnp.zeros((4, 8, LANES), F32)
    xpad[:, 0:8, :] = jnp.zeros((4, 8, LANES), F32)
    pairs[0:32, :] = jnp.zeros((32, LANES), F32)
    sums[0:32, :] = jnp.zeros((32, LANES), F32)

    lane = lax.broadcasted_iota(jnp.int32, (64, SIDE), 1)

    def shape(half, halo):
        turned = cols[...].T
        part = slice(half * LANES, (half + 1) * LANES)
        for block in range(4):
            rows = slice(64 * block, 64 * block + 64)
            shaped = []
            for stream in range(3):
                now = feat[stream, rows, :].astype(F32)
                one = pltpu.roll(now, 1, 1)
                two = pltpu.roll(now, 2, 1)
                if halo:
                    last = turned[rows, 16 + 2 * stream + 1 : 16 + 2 * stream + 2]
                    older = turned[rows, 16 + 2 * stream : 16 + 2 * stream + 1]
                    one = jnp.where(lane == 0, last, one)
                    two = jnp.where(lane == 0, older, jnp.where(lane == 1, last, two))
                tap = [turned[rows, 3 * stream + j : 3 * stream + j + 1] for j in range(3)]
                shaped.append(
                    tap[0] * now[:, part] + tap[1] * one[:, part] + tap[2] * two[:, part]
                )
            gate[rows, part] = shaped[0].astype(BF16)
            kv[rows, part] = (shaped[1] * shaped[2]).astype(BF16)

    shape(1, False)

    pl.semaphore_wait(barrier, len(peers))

    sent = []
    halo_copy = remote(halo_out, halo_in, halo_sem.at[0], halo_sem.at[1], after)
    halo_copy.start()
    bias_copy = remote(bias_out, bias_in, bias_sem.at[0], bias_sem.at[1], across(z_hi))
    bias_copy.start()

    sent.extend([halo_copy, bias_copy])

    def plane_exchange(src, dst, which):
        copies = []
        for step in PLACES:
            to, device = plane(step)
            copy = remote(
                src.at[pl.ds(pl.multiple_of(to * 16, 16), 16)],
                dst.at[pl.ds(pl.multiple_of(here * 16, 16), 16)],
                xy_send.at[which, step], xy_recv.at[which, step], device,
            )
            copy.start()
            copies.append(copy)
        mine = pl.ds(pl.multiple_of(here * 16, 16), 16)
        dst[mine, :] = src[mine, :]
        sent.extend(copies)
        return copies

    def across_exchange(src, dst, send, recv, first, rows):
        copies = []
        for step in (2, 1, 3, 0):
            to = lax.rem(z_hi + step, 4)
            copy = remote(
                src.at[pl.ds(pl.multiple_of(to * 64 + first, 16), rows)],
                dst.at[pl.ds(pl.multiple_of(z_hi * 64 + first, 16), rows)],
                send.at[step], recv.at[step], across(to),
            )
            copy.start()
            copies.append(copy)
        sent.extend(copies)
        return copies

    def arrived(copies):
        for copy in copies:
            copy.wait_recv()

    def spread(src, dst, start, ch):
        for zs in range(4):
            tile = src[pl.ds(zs * 64 + ch * 16, 16), :].astype(F32)
            for xs in range(4):
                for half in range(2):
                    first = start + (xs * 16 + zs * 4) * 2 + half
                    dst[ch, pl.ds(first, 4, stride=2), :] = tile[
                        4 * xs : 4 * xs + 4, half * LANES : (half + 1) * LANES
                    ]

    filt_across = across_exchange(filt_pre, filt_zr, z_send, z_recv, 0, 64)

    halo_copy.wait_recv()
    seen = jnp.where(context > 0, 1.0, 0.0)
    cols[16:32, :] = halo_in[...].astype(F32) * seen
    shape(0, True)

    kv_plane = plane_exchange(kv, kv_xy, 1)
    arrived(kv_plane)
    swap_blocks(kv_xy, kv_zs)
    kv_across = [
        across_exchange(kv_zs, kv_zr, kv_send.at[ch], kv_recv.at[ch], 16 * ch, 16)
        for ch in range(4)
    ]

    arrived(filt_across)
    swap_blocks(filt_zr, filt_zs)
    arrived(plane_exchange(filt_zs, filt_xy, 0))
    swap_blocks(filt_xy, filt_all)
    for ch in range(4):
        spread(filt_all, hpad, 8, ch)

    low = lax.broadcasted_iota(jnp.int32, (16, LANES), 1) < 64
    for ch in range(4):
        for a in range(4):
            one = hpad[ch, pl.ds(8 + 32 * a, 16), :]
            two = hpad[ch, pl.ds(24 + 32 * a, 16), :]
            even = jnp.where(low, one, pltpu.roll(two, 64, 1))
            odd = jnp.where(low, pltpu.roll(one, 64, 1), two)
            ahead[ch, pl.ds(32 * a, 16, stride=2), :] = even
            ahead[ch, pl.ds(32 * a + 1, 16, stride=2), :] = odd
            behind[ch, pl.ds(32 * a + 1, 16, stride=2), :] = pltpu.roll(even, 64, 1)
            behind[ch, pl.ds(32 * a + 2, 16, stride=2), :] = pltpu.roll(odd, 64, 1)
        for a in range(4):
            one = hpad[ch, pl.ds(23 + 32 * a, 1), :]
            two = hpad[ch, pl.ds(7 + 32 * a, 1), :]
            behind[ch, pl.ds(32 * a, 1), :] = jnp.where(low[:1], pltpu.roll(one, 64, 1), two)
    lane = lax.broadcasted_iota(jnp.int32, (64, LANES), 1)
    down = lax.broadcasted_iota(jnp.int32, (64, LANES), 0)
    keep = lax.rem(lane, 64) + down < 64

    def build(index, carry):
        ch = lax.div(index, 32)
        b = lax.rem(index, 32)
        for a in range(4):
            block = jnp.where(
                keep,
                jnp.broadcast_to(ahead[ch, pl.ds(32 * a + b, 1), :], (64, LANES)),
                jnp.broadcast_to(behind[ch, pl.ds(32 * a + b, 1), :], (64, LANES)),
            )
            block = pltpu.roll(block, 0, 1, stride=1, stride_axis=0)
            toep[ch, pl.ds(pl.multiple_of(b * 64, 64), 64), pl.ds(a * LANES, LANES)] = (
                block.astype(BF16)
            )
        return carry

    lax.fori_loop(0, 128, build, 0)

    bias_copy.wait_recv()
    spot = lax.broadcasted_iota(jnp.int32, (1, SIDE), 1)
    first_lanes = lax.broadcasted_iota(jnp.int32, (LANES, LANES), 1) < 64
    back = []
    for ch in range(4):
        arrived(kv_across[ch])
        spread(kv_zr, xpad, 8, ch)
        own_row = xpad[ch, pl.ds(8, LANES), :]
        row_before = xpad[ch, pl.ds(7, LANES), :]
        pairs[pl.ds(32, LANES, stride=2), :] = jnp.where(first_lanes, own_row, row_before)
        pairs[pl.ds(33, LANES, stride=2), :] = pltpu.roll(own_row, 64, 1)
        for b in range(16):
            xs_buf[:, pl.ds(b * LANES, LANES)] = pairs[pl.ds(32 - 2 * b, SIDE), :].astype(BF16)
        upper = jnp.dot(xs_buf[...], toep[ch, :, pl.ds(0, SIDE)], preferred_element_type=F32)
        lower = jnp.dot(
            xs_buf[pl.ds(0, LANES), :], toep[ch, :, pl.ds(SIDE, SIDE)],
            preferred_element_type=F32,
        )
        sums[pl.ds(32, SIDE), :] = upper[:, :LANES]
        sums[pl.ds(96, 192), :] += upper[:192, LANES:]
        sums[pl.ds(160, LANES), :] += lower[:, :LANES]
        sums[pl.ds(224, 64), :] += lower[:64, LANES:]
        folded[...] = sums[pl.ds(32, SIDE), :] + pltpu.roll(sums[pl.ds(0, SIDE), :], 64, 1)
        total = jnp.where(
            first_lanes,
            folded[pl.ds(0, LANES, stride=2), :],
            pltpu.roll(folded[pl.ds(1, LANES, stride=2), :], 64, 1),
        )
        channel = here * 16 + z_hi * 4 + ch
        bias = jnp.sum(jnp.where(spot == channel, bias_in[...], 0.0), axis=1, keepdims=True)
        ypad[...] = total + bias * own_row
        for zs in range(4):
            for xs in range(4):
                for half in range(2):
                    first = (xs * 16 + zs * 4) * 2 + half
                    piece[pl.ds(4 * xs, 4), pl.ds(half * LANES, LANES)] = ypad[
                        pl.ds(first, 4, stride=2), :
                    ]
            mix_zs[pl.ds(zs * 64 + ch * 16, 16), :] = piece[...].astype(BF16)
        back += across_exchange(
            mix_zs, mix_zr, back_send.at[ch], back_recv.at[ch], 16 * ch, 16
        )

    arrived(back)
    swap_blocks(mix_zr, mix_ss)
    arrived(plane_exchange(mix_ss, mix, 2))

    gated = (gate[...].astype(F32) * mix[...].astype(F32)).astype(BF16).astype(F32)
    gated_t[...] = gated.T.astype(BF16)
    loads[2].wait()

    def sib_copy(d):
        return remote(sib_out.at[d], sib_in.at[d], sib_send.at[d], sib_recv.at[d], sibling)

    for d in (7, 0, 6, 1, 5, 2, 4, 3):
        theirs = pl.ds(pl.multiple_of((2 * d + 1 - core) * SIDE, SIDE), SIDE)
        mine = pl.ds(pl.multiple_of((2 * d + core) * SIDE, SIDE), SIDE)
        sib_out[d] = jnp.dot(gated_t[...], w[:, theirs], preferred_element_type=F32).astype(BF16)
        sib_copy(d).start()
        own[d] = jnp.dot(gated_t[...], w[:, mine], preferred_element_type=F32)

    size = SIDE // PARTS

    def rows_of(n):
        return pl.ds(pl.multiple_of(lax.rem(n, PARTS) * size, size), size)

    quarter = lax.rem(z_lo, 4)

    def right_copy(n):
        d = 7 - lax.div(n, PARTS)
        return remote(
            right_out.at[d, rows_of(n)], right_in.at[d, rows_of(n)],
            right_send.at[n], right_recv.at[n], right,
        )

    def right_jump(n, d):
        return remote(
            right_out.at[7 - lax.div(n, PARTS), rows_of(n)], right_far.at[rows_of(n)],
            right_send.at[n], right_recv.at[STEPS + lax.rem(n, PARTS)], along(d),
        )

    def left_copy(n):
        d = lax.div(n, PARTS)
        return remote(
            left_out.at[d, rows_of(n)], left_in.at[d, rows_of(n)],
            left_send.at[n], left_recv.at[n], left,
        )

    def left_jump(n, d):
        return remote(
            left_out.at[lax.div(n, PARTS), rows_of(n)], left_far.at[rows_of(n)],
            left_send.at[n], left_recv.at[STEPS + lax.rem(n, PARTS)], along(d),
        )

    def pass_on(n, d, first, jumps, copy, jump, came, going):
        rows = rows_of(n)

        @pl.when(lax.rem(n, PARTS) == 0)
        def _():
            sib_copy(d).wait_recv()

        @pl.when(first)
        def _():
            going[d, rows, :] = (own[d, rows, :] + sib_in[d, rows, :].astype(F32)).astype(BF16)

        @pl.when(jnp.logical_not(first))
        def _():
            copy.wait_recv()
            going[d, rows, :] = (
                own[d, rows, :] + sib_in[d, rows, :].astype(F32) + came[d, rows, :].astype(F32)
            ).astype(BF16)

        @pl.when(jumps)
        def _():
            jump.start()

        @pl.when(jnp.logical_not(jumps))
        def _():
            copy.start()

    def reduce_step(moment, carry):
        n = moment - quarter * LAG

        @pl.when((n >= 0) & (n < (7 - z_lo) * PARTS))
        def _():
            d = 7 - lax.div(n, PARTS)
            pass_on(
                n, d, (quarter == 0) | ((z_lo == 2) & (d == 4)),
                ((z_lo == 3) & (d > 4)) | ((z_lo == 1) & (d == 4)),
                right_copy(n), right_jump(n, d), right_in, right_out,
            )

        m = moment - (3 - quarter) * LAG

        @pl.when((m >= 0) & (m < z_lo * PARTS))
        def _():
            d = lax.div(m, PARTS)
            pass_on(
                m, d, (quarter == 3) | ((z_lo == 5) & (d == 3)),
                ((z_lo == 4) & (d < 3)) | ((z_lo == 6) & (d == 3)),
                left_copy(m), left_jump(m, d), left_in, left_out,
            )

        return carry

    lax.fori_loop(0, STEPS + 3 * LAG, reduce_step, 0)

    sib_copy(z_lo).wait_recv()
    own[z_lo] = own[z_lo] + sib_in[z_lo].astype(F32)

    @pl.when(z_lo > 0)
    def _():
        for part in range(PARTS):
            right_copy((7 - z_lo) * PARTS + part).wait_recv()
        own[z_lo] = own[z_lo] + right_in[z_lo].astype(F32)

    @pl.when(z_lo < 7)
    def _():
        for part in range(PARTS):
            left_copy(z_lo * PARTS + part).wait_recv()
        own[z_lo] = own[z_lo] + left_in[z_lo].astype(F32)

    @pl.when(z_lo > 3)
    def _():
        for part in range(PARTS):
            right_jump(part, z_lo).wait_recv()
        own[z_lo] = own[z_lo] + right_far[...].astype(F32)

    @pl.when(z_lo < 4)
    def _():
        for part in range(PARTS):
            left_jump(part, z_lo).wait_recv()
        own[z_lo] = own[z_lo] + left_far[...].astype(F32)

    out_ref[...] = own[z_lo].astype(BF16)

    for copy in sent:
        copy.wait_send()
    for d in range(8):
        sib_copy(d).wait_send()

    def close(n, carry):
        @pl.when(n < (7 - z_lo) * PARTS)
        def _():
            right_copy(n).wait_send()

        @pl.when(n < z_lo * PARTS)
        def _():
            left_copy(n).wait_send()

        return carry

    lax.fori_loop(0, STEPS, close, 0)


def local(features, short_taps, long_filter, skip_bias, out_weight):
    vmem = pl.BlockSpec(memory_space=pltpu.VMEM)
    anywhere = pl.BlockSpec(memory_space=pl.ANY)
    square = pltpu.VMEM((SIDE, SIDE), BF16)
    dma = pltpu.SemaphoreType.DMA
    return pl.pallas_call(
        kernel,
        out_shape=jax.ShapeDtypeStruct((SIDE, SIDE), BF16),
        in_specs=[anywhere] * 5,
        out_specs=vmem,
        scratch_shapes=[
            pltpu.VMEM((3, SIDE, SIDE), BF16),
            pltpu.VMEM((3, 3, SIDE), F32),
            square,
            pltpu.VMEM((1, SIDE), F32),
            pltpu.VMEM((SIDE, 16 * SIDE), BF16),
            pltpu.VMEM((LANES, SIDE), F32),
            pltpu.VMEM((16, SIDE), BF16),
            pltpu.VMEM((16, SIDE), BF16),
            pltpu.VMEM((1, SIDE), F32),
            square, square,
            square, square, square, square, square,
            square, square, square,
            square, square, square, square,
            pltpu.VMEM((2, SIDE, LANES), F32),
            pltpu.VMEM((4, 136, LANES), F32),
            pltpu.VMEM((4, LANES, LANES), F32),
            pltpu.VMEM((4, 136, LANES), F32),
            pltpu.VMEM((4, 136, LANES), F32),
            pltpu.VMEM((32 + SIDE, LANES), F32),
            pltpu.VMEM((32 + SIDE, LANES), F32),
            pltpu.VMEM((SIDE, LANES), F32),
            pltpu.VMEM((LANES, LANES), F32),
            pltpu.VMEM((16, SIDE), F32),
            pltpu.VMEM((SIDE, 2048), BF16),
            pltpu.VMEM((4, 2048, 512), BF16),
            square,
            pltpu.VMEM((8, SIDE, SIDE), BF16),
            pltpu.VMEM((8, SIDE, SIDE), BF16),
            pltpu.VMEM((8, SIDE, SIDE), F32),
            pltpu.VMEM((8, SIDE, SIDE), BF16), pltpu.VMEM((8, SIDE, SIDE), BF16), square,
            pltpu.VMEM((8, SIDE, SIDE), BF16), pltpu.VMEM((8, SIDE, SIDE), BF16), square,
            dma((5,)), dma((2,)), dma((2,)),
            dma((3, 16)), dma((3, 16)),
            dma((4,)), dma((4,)),
            dma((4, 4)), dma((4, 4)),
            dma((4, 4)), dma((4, 4)),
            dma((8,)), dma((8,)),
            dma((STEPS,)), dma((STEPS + PARTS,)), dma((STEPS,)), dma((STEPS + PARTS,)),
        ],
        compiler_params=pltpu.CompilerParams(
            collective_id=0, has_side_effects=True, vmem_limit_bytes=60 << 20
        ),
        cost_estimate=pl.CostEstimate(
            flops=4 * 10**9, bytes_accessed=3 * 10**6, transcendentals=0
        ),
        name="hyena_operator",
    )(features, short_taps, long_filter, skip_bias.reshape(1, SIDE), out_weight)


def solution(mesh):
    placed = (
        P(None, "tensor", "context"),
        P(None, None, "tensor"),
        P("tensor", "context"),
        P("tensor"),
        P("tensor", None),
    )
    return jax.shard_map(
        local, mesh=mesh, in_specs=placed, out_specs=P("context", "tensor"), check_vma=False
    )
```
